128 devices in a mesh: dp: 8 (over z, x_lo), tensor: 8 (over x_hi, y), pre: 2 (over core).
Axes of the slice: x: 4 (x_hi: 2, x_lo: 2; x = x_hi * 2 + x_lo), y: 4, z: 4, core: 2. Of those that a mesh axis runs over, the one named last changes fastest.
Arguments:
- tokens: bfloat16 [8192, 4096], P('dp', ('tensor', 'pre')), may hold values from -6 to 6
- weight: bfloat16 [4096, 16384], P('dp', ('tensor', 'pre')), may hold values from -0.09375 to 0.09375
- cotangent: bfloat16 [8192, 16384], P('dp', ('tensor', 'pre')), may hold values from -6 to 6
- left_stats: float32 [8, 32, 512, 512], P('dp', ('tensor', 'pre')), as said below
- right_stats: float32 [8, 32, 512, 512], P('dp', ('tensor', 'pre')), as said below
Outputs:
- tokens_grad: bfloat16 [8192, 4096], P('dp', ('tensor', 'pre'))
- update: bfloat16 [4096, 16384], P('dp', ('tensor', 'pre'))
- left_new: float32 [8, 32, 512, 512], P('dp', ('tensor', 'pre'))
- right_new: float32 [8, 32, 512, 512], P('dp', ('tensor', 'pre'))
The draws below stay inside these ranges and needn't reach their ends.
Inputs may be any that keep to these rules, and one draw needn't show every extreme that they name: `left_stats`: each block is symmetric positive definite. `right_stats`: each block is symmetric positive definite.
All inputs are finite; a program needn't handle non-finite values.
Results may differ from the reference program's by a relative error of at most 0.02.
Values may be sent and summed in bfloat16 or wider, within the bound.
A program may use at most 192 MiB of HBM per device.

```python
import jax
import jax.numpy as jnp
from jax import lax

D = 4096
FF = 16384
BLOCK = 512
ITERS = 3
TOK_DEV = 1024
TOKENS = 8192
ROW_BLOCKS = 8
COL_BLOCKS = 32
N_DP = 8
N_TENSOR = 8
N_PRE = 2


def symmetric_blocks(key, upper):
    first_key, second_key = jax.random.split(key)
    shape = (D // BLOCK, FF // BLOCK, BLOCK, BLOCK)
    identity_mat = jnp.eye(BLOCK, dtype=jnp.float32)
    off_part = jax.random.uniform(first_key, shape, jnp.float32, -0.1, 0.1) / BLOCK
    off_part = (off_part + jnp.swapaxes(off_part, -1, -2)) * (1.0 - identity_mat)
    diagonal = jnp.exp(jax.random.uniform(second_key, shape[:-1], jnp.float32, jnp.log(0.25), jnp.log(upper)))
    return off_part + diagonal[..., None] * identity_mat


def draw_left_stats(key, part):
    key = jax.random.fold_in(key, 11)
    upper = 2.5
    return symmetric_blocks(key, upper)


def draw_right_stats(key, part):
    key = jax.random.fold_in(key, 23)
    upper = 2.5
    return symmetric_blocks(key, upper)


def with_spikes(values, own_key, source, target, blocks, factor):
    def block_of(position):
        return (jnp.arange(values.shape[position]) // (values.shape[position] // blocks)).reshape((-1,) + (1,) * (values.ndim - 1 - position))

    one_side = jax.random.permutation(own_key, blocks)[block_of(target)]
    other_side = (block_of(target) + blocks // 2) % blocks
    return jnp.where((block_of(source) == one_side) | (block_of(source) == other_side), factor * values, values)


def shard_levels(key, shape, cuts, low, top_value):
    gain = 1.0
    for dim, parts in cuts:
        steps = jax.random.uniform(jax.random.fold_in(jax.random.fold_in(key, 6), dim), (parts,), jnp.float32, low / len(cuts), top_value / len(cuts))
        gain = gain * jnp.repeat(jnp.exp(steps), shape[dim] // parts).reshape((-1,) + (1,) * (len(shape) - 1 - dim))
    return gain


def centred(own_key, shape, scale, most, pieces=(), held_as=jnp.bfloat16):
    loudness = shard_levels(own_key, shape, pieces, -0.22, 0.18) if pieces else 1.0
    array = jax.random.normal(own_key, shape, jnp.float32) * scale * loudness
    return jnp.minimum(jnp.maximum(array, -most), most).astype(held_as)


def noise_with(rng, dims, scale, reach, cuts, heavy, kind=jnp.bfloat16):
    values = scale * jax.random.normal(rng, dims, jnp.float32)
    if cuts:
        values = values * shard_levels(rng, dims, cuts, -0.22, 0.18)
    return jnp.clip(with_spikes(values, jax.random.fold_in(rng, 3), *heavy), -reach, reach).astype(kind)


def setup_inputs(seed: int = 0) -> dict:
    key_of = jax.random.split(jax.random.key(seed), 6)
    tokens = noise_with(key_of[0], (TOKENS, D), 1.0, 6.0, ((0, 8), (1, 16)), (0, 1, 16, 2.0))
    weight = centred(key_of[1], (D, FF), D ** -0.5, 0.09375, ((0, 8), (1, 16)))
    cotangent = centred(key_of[2], (TOKENS, FF), 1.0, 6.0, ((0, 8), (1, 16)))
    left_stats = draw_left_stats(jax.random.fold_in(key_of[5], 71), 0)
    right_stats = draw_right_stats(jax.random.fold_in(key_of[5], 71), 0)
    return dict(tokens=tokens, weight=weight, cotangent=cotangent, left_stats=left_stats, right_stats=right_stats)


decay_rate = 0.5
ridge_share = 0.05
epsilon = 1e-06

def gelu_slope(values):
    return 0.5 * (1.0 + lax.erf(values * 0.7071067811865476)) + values * jnp.exp(-0.5 * values * values) * 0.3989422804014327

def matmul_high(left, right):
    return jnp.einsum('kij,kjl->kil', left, right, precision=lax.Precision.HIGHEST)

def newton_roots(statistic):
    size = statistic.shape[-1]
    identity_mat = jnp.eye(size, dtype=jnp.float32)
    trace_val = lax.optimization_barrier(jnp.sum(statistic * identity_mat, axis=(1, 2), keepdims=True))
    regular = statistic + ridge_share * (trace_val / size) * identity_mat
    norm_scale = jnp.sqrt(lax.optimization_barrier(jnp.sum(regular * regular, axis=(1, 2), keepdims=True))) / 4.0
    current = regular / norm_scale
    inverse_root = identity_mat
    for sweep in range(ITERS):
        step_mat = (5.0 * identity_mat - current) / 4.0
        if sweep == 0:
            inverse_root = norm_scale ** (-0.25) * step_mat
        else:
            inverse_root = matmul_high(inverse_root, step_mat)
        if sweep + 1 < ITERS:
            square = matmul_high(step_mat, step_mat)
            current = matmul_high(matmul_high(square, square), current)
    return inverse_root.astype(jnp.bfloat16)

def precondition(grad_blocks, left_old, right_old):
    size = grad_blocks.shape[-1]
    left_new = decay_rate * left_old + (1.0 - decay_rate) / size * jnp.einsum('kij,klj->kil', grad_blocks, grad_blocks, precision=lax.Precision.HIGHEST)
    right_new = decay_rate * right_old + (1.0 - decay_rate) / size * jnp.einsum('kji,kjl->kil', grad_blocks, grad_blocks, precision=lax.Precision.HIGHEST)
    left_root = newton_roots(left_new)
    right_root = newton_roots(right_new)
    grad_half = grad_blocks.astype(jnp.bfloat16)
    left_part = jnp.einsum('kij,kjl->kil', left_root, grad_half, preferred_element_type=jnp.float32).astype(jnp.bfloat16)
    raw = jnp.einsum('kij,kjl->kil', left_part, right_root, preferred_element_type=jnp.float32)
    grad_rms = jnp.sqrt(lax.optimization_barrier(jnp.mean(grad_blocks * grad_blocks, axis=(1, 2), keepdims=True)))
    raw_rms = jnp.sqrt(lax.optimization_barrier(jnp.mean(raw * raw, axis=(1, 2), keepdims=True)) + epsilon)
    return ((raw * grad_rms / raw_rms).astype(jnp.bfloat16), left_new, right_new)

def reference(tokens, weight, cotangent, left_stats, right_stats):
    groups = N_TENSOR * N_PRE
    col_width = FF // groups
    hidden = jnp.dot(tokens, weight, preferred_element_type=jnp.float32)
    hidden_grad = (cotangent.astype(jnp.float32) * gelu_slope(hidden)).astype(jnp.bfloat16)
    grad_cols = hidden_grad.reshape(TOKENS, groups, col_width).transpose(1, 0, 2)
    weight_cols = weight.reshape(D, groups, col_width).transpose(1, 0, 2)

    def add_input(carry, pair):
        partial_sum = lax.dot_general(pair[0], pair[1], (((1,), (1,)), ((), ())), preferred_element_type=jnp.float32)
        return (carry + partial_sum.astype(jnp.bfloat16).astype(jnp.float32), None)
    input_sum, unused = lax.scan(add_input, jnp.zeros((TOKENS, D), jnp.float32), (grad_cols, weight_cols))
    tokens_grad = input_sum.astype(jnp.bfloat16)
    grad_scale = float(TOKENS) ** (-0.5)
    token_groups = tokens.reshape(N_DP, TOK_DEV, D)
    hidden_groups = hidden_grad.reshape(N_DP, TOK_DEV, FF)

    def add_grad(carry, pair):
        partial_sum = lax.dot_general(pair[0], pair[1], (((0,), (0,)), ((), ())), preferred_element_type=jnp.float32) * grad_scale
        return (carry + partial_sum.astype(jnp.bfloat16).astype(jnp.float32), None)
    grad, unused = lax.scan(add_grad, jnp.zeros((D, FF), jnp.float32), (token_groups, hidden_groups))
    blocks = grad.reshape(ROW_BLOCKS, BLOCK, COL_BLOCKS, BLOCK).transpose(0, 2, 1, 3)
    update_blocks, left_new, right_new = lax.map(lambda triple: precondition(triple[0], triple[1], triple[2]), (blocks, left_stats, right_stats))
    update = update_blocks.transpose(0, 2, 1, 3).reshape(D, FF)
    return (tokens_grad, update, left_new, right_new)
```

```python
import jax
import jax.numpy as jnp
from jax import lax
from jax.sharding import PartitionSpec as P

ITERS = 3


decay_rate = 0.5
ridge_share = 0.05
epsilon = 1e-06


def gelu_slope(values):
    return (
        0.5 * (1.0 + lax.erf(values * 0.7071067811865476))
        + values * jnp.exp(-0.5 * values * values) * 0.3989422804014327
    )


def product(left, right):
    return jnp.einsum(
        "kij,kjl->kil",
        left.astype(jnp.bfloat16),
        right.astype(jnp.bfloat16),
        preferred_element_type=jnp.float32,
    )


def newton_roots(statistic):
    size = statistic.shape[-1]
    identity_mat = jnp.eye(size, dtype=jnp.float32)
    trace_val = jnp.sum(statistic * identity_mat, axis=(1, 2), keepdims=True)
    regular = statistic + ridge_share * (trace_val / size) * identity_mat
    norm_scale = jnp.sqrt(jnp.sum(regular * regular, axis=(1, 2), keepdims=True)) / 4.0
    first = regular / norm_scale
    square = product(first, first)
    step_zero = 1.25 * identity_mat - 0.25 * first
    step_zero_sq = 1.5625 * identity_mat - 0.625 * first + 0.0625 * square
    fourth = product(step_zero_sq, step_zero_sq)
    crossed = 1.25 * first - 0.25 * square
    root_two = 1.25 * step_zero - 0.25 * product(fourth, crossed)
    two_sq = product(root_two, root_two)
    two_fourth = product(two_sq, two_sq)
    two_crossed = product(root_two, first)
    root_three = 1.25 * root_two - 0.25 * product(two_fourth, two_crossed)
    return (norm_scale ** (-0.25) * root_three).astype(jnp.bfloat16)


def shards(tokens, weight, cotangent, left_stats, right_stats):
    features_all = lax.all_gather(tokens, ("tensor", "pre"), axis=1, tiled=True)
    tok_rows = tokens.shape[0]
    weight_all = lax.all_gather(weight, "dp", axis=0, tiled=True)
    hidden = jnp.dot(
        features_all,
        weight_all,
        preferred_element_type=jnp.float32,
    )
    hidden_grad = (cotangent.astype(jnp.float32) * gelu_slope(hidden)).astype(jnp.bfloat16)
    input_part = lax.dot_general(
        hidden_grad,
        weight_all,
        (((1,), (1,)), ((), ())),
        preferred_element_type=jnp.float32,
    )
    tokens_grad = lax.psum_scatter(
        input_part.astype(jnp.bfloat16), ("tensor", "pre"), scatter_dimension=1, tiled=True
    )
    dp_count = lax.axis_size("dp")
    grad_scale = float(tok_rows * dp_count) ** (-0.5)
    grad_part = (
        lax.dot_general(
            features_all, hidden_grad, (((0,), (0,)), ((), ())), preferred_element_type=jnp.float32
        )
        * grad_scale
    )
    grad = lax.psum_scatter(
        grad_part.astype(jnp.bfloat16), "dp", scatter_dimension=0, tiled=True
    ).astype(jnp.float32)
    row_count = left_stats.shape[0]
    col_count = left_stats.shape[1]
    size = left_stats.shape[2]
    count = row_count * col_count
    blocks = (
        grad.reshape(row_count, size, col_count, size)
        .transpose(0, 2, 1, 3)
        .reshape(count, size, size)
    )
    left_old = left_stats.reshape(count, size, size)
    right_old = right_stats.reshape(count, size, size)
    left_new = decay_rate * left_old + (1.0 - decay_rate) / size * product(
        blocks, blocks.transpose(0, 2, 1)
    )
    right_new = decay_rate * right_old + (1.0 - decay_rate) / size * product(
        blocks.transpose(0, 2, 1), blocks
    )
    statistic = jnp.concatenate([left_new, right_new], axis=0)
    roots_all = newton_roots(statistic)
    left_root = roots_all[:count]
    right_root = roots_all[count:]
    grad_half = blocks.astype(jnp.bfloat16)
    left_part = jnp.einsum(
        "kij,kjl->kil", left_root, grad_half, preferred_element_type=jnp.float32
    ).astype(jnp.bfloat16)
    raw = jnp.einsum("kij,kjl->kil", left_part, right_root, preferred_element_type=jnp.float32)
    grad_rms = jnp.sqrt(jnp.mean(blocks * blocks, axis=(1, 2), keepdims=True))
    raw_rms = jnp.sqrt(jnp.mean(raw * raw, axis=(1, 2), keepdims=True) + epsilon)
    update_blocks = (raw * grad_rms / raw_rms).astype(jnp.bfloat16)
    update = (
        update_blocks.reshape(row_count, col_count, size, size)
        .transpose(0, 2, 1, 3)
        .reshape(row_count * size, col_count * size)
    )
    left_out = left_new.reshape(row_count, col_count, size, size)
    right_out = right_new.reshape(row_count, col_count, size, size)
    return (tokens_grad, update, left_out, right_out)


def solution(mesh):
    return jax.shard_map(
        shards,
        mesh=mesh,
        in_specs=(
            P("dp", ("tensor", "pre")),
            P("dp", ("tensor", "pre")),
            P("dp", ("tensor", "pre")),
            P("dp", ("tensor", "pre"), None, None),
            P("dp", ("tensor", "pre"), None, None),
        ),
        out_specs=(
            P("dp", ("tensor", "pre")),
            P("dp", ("tensor", "pre")),
            P("dp", ("tensor", "pre"), None, None),
            P("dp", ("tensor", "pre"), None, None),
        ),
        check_vma=False,
    )
```

```python
import jax
import jax.numpy as jnp
from jax import lax
from jax.experimental import pallas as pl
from jax.experimental.pallas import tpu as pltpu
from jax.sharding import PartitionSpec as P

MESH = pl.DeviceIdType.MESH
F32 = jnp.float32
BF16 = jnp.bfloat16

TOK = 1024
D = 4096
BLK = 512
COLS = 1024
FEAT = 256

decay_rate = 0.5
ridge_share = 0.05
epsilon = 1e-06
grad_scale = float(8192) ** (-0.5)

XA = (0, 192)
ZA = (192, 64)
ZB = (256, 64)
XB = (320, 192)
ZZ = (192, 128)
HA = (0, 256)
HB = (256, 256)
NSEM = 160


def dot(a, b):
    return jnp.dot(a, b, preferred_element_type=F32)


def gelu_slope(values):
    return (
        0.5 * (1.0 + lax.erf(values * 0.7071067811865476))
        + values * jnp.exp(-0.5 * values * values) * 0.3989422804014327
    )


def add_rows(dst, sources, rows, chunk=32):
    def body(i, carry):
        at = pl.ds(pl.multiple_of(i * chunk, chunk), chunk)
        total = sources[0][at, :].astype(F32)
        for source in sources[1:]:
            total = total + source[at, :].astype(F32)
        dst[at, :] = total.astype(dst.dtype)
        return carry

    lax.fori_loop(0, rows // chunk, body, 0)


def exchange_kernel(
    tok_ref, w_ref, cot_ref, tg_ref, gt_ref,
    wf, tok, hg, hgt, hid, part,
    s1, s1z, s2, s2z, rz, rx, sib, t1, t2, tx,
    ss, rs, ls,
):
    dp = lax.axis_index("dp")
    tn = lax.axis_index("tensor")
    c = lax.axis_index("pre")
    z, l = lax.div(dp, 2), lax.rem(dp, 2)
    xh, y = lax.div(tn, 4), lax.rem(tn, 4)
    m = 1 - l
    up, um, u2 = lax.rem(z + 1, 4), lax.rem(z + 3, 4), lax.rem(z + 2, 4)
    yp, ym, y2 = lax.rem(y + 1, 4), lax.rem(y + 3, 4), lax.rem(y + 2, 4)
    oh, oc = 1 - xh, 1 - c
    dev_zp, dev_zm = (up * 2 + l, tn, c), (um * 2 + l, tn, c)
    dev_x = (z * 2 + m, tn, c)
    dev_yp, dev_ym = (dp, xh * 4 + yp, c), (dp, xh * 4 + ym, c)
    dev_h = (dp, oh * 4 + y, c)
    dev_c = (dp, tn, oc)

    barrier = pltpu.get_barrier_semaphore()
    for dev in (dev_zp, dev_zm, dev_x, dev_yp, dev_ym, dev_h, dev_c):
        pl.semaphore_signal(barrier, inc=1, device_id=dev, device_id_type=MESH)
    pl.semaphore_wait(barrier, 7)

    copies = []

    def send(src, dst, dev):
        k = len(copies)
        copy = pltpu.make_async_remote_copy(
            src_ref=src, dst_ref=dst, send_sem=ss.at[k], recv_sem=rs.at[k],
            device_id=dev, device_id_type=MESH,
        )
        copy.start()
        copies.append(copy)
        return copy

    def got(*several):
        for copy in several:
            copy.wait_recv()

    def rows_of(zi, li, rows):
        return pl.ds(pl.multiple_of((zi * 2 + li) * BLK + rows[0], 64), rows[1])

    def wpart(zi, li, rows, h):
        return wf.at[rows_of(zi, li, rows), pl.ds(h * BLK, BLK)]

    def wsend(zi, li, rows, h, dev):
        ref = wpart(zi, li, rows, h)
        return send(ref, ref, dev)

    wstate = [dict(), dict()]

    def w_own(h):
        q = wstate[h]

        def own(rows, dev):
            return send(
                w_ref.at[pl.ds(rows[0], rows[1]), pl.ds(h * BLK, BLK)],
                wpart(z, l, rows, h), dev,
            )

        q["xa"], q["xb"] = own(XA, dev_x), own(XB, dev_x)
        q["pa"], q["mb"] = own(HA, dev_zp), own(HB, dev_zm)
        q["pb"], q["ma"] = own(HB, dev_zp), own(HA, dev_zm)
        q["xz"] = own(ZZ, dev_x)

    def w_partner(h):
        q = wstate[h]
        got(q["xa"])
        q["ppa"] = wsend(z, m, XA, h, dev_zp)
        q["pma"] = wsend(z, m, XA, h, dev_zm)
        got(q["xb"])
        q["pmb"] = wsend(z, m, XB, h, dev_zm)
        q["ppb"] = wsend(z, m, XB, h, dev_zp)

    def w_forward_own(h):
        q = wstate[h]
        got(q["pa"])
        q["fa"] = wsend(um, l, HA, h, dev_zp)
        got(q["mb"])
        q["fb"] = wsend(up, l, HB, h, dev_zm)
        got(q["pb"])
        q["xzm"] = wsend(um, l, ZZ, h, dev_x)
        got(q["ma"])
        q["xzp"] = wsend(up, l, ZZ, h, dev_x)

    def w_forward_partner(h):
        q = wstate[h]
        got(q["ppa"])
        q["fpa"] = wsend(um, m, XA, h, dev_zp)
        got(q["pmb"])
        q["fpb"] = wsend(up, m, XB, h, dev_zm)

    def w_last(h):
        q = wstate[h]
        got(q["fa"])
        q["x2a"] = wsend(u2, l, ZA, h, dev_x)
        got(q["fb"])
        q["x2b"] = wsend(u2, l, ZB, h, dev_x)

    def w_done(h):
        q = wstate[h]
        got(*(q[k] for k in ("xz", "ppb", "pma", "xzm", "xzp", "fpa", "fpb", "x2a", "x2b")))

    TA, TB = pl.ds(0, TOK // 2), pl.ds(TOK // 2, TOK // 2)
    ALL = pl.ds(0, TOK)

    def tcols(hi, yi, ci):
        return pl.ds(pl.multiple_of(((hi * 4 + yi) * 2 + ci) * FEAT, FEAT), FEAT)

    def tsend(hi, yi, rows, dev):
        ref = tok.at[rows, tcols(hi, yi, c)]
        return send(ref, ref, dev)

    tq = {}

    def t_own():
        def own(rows, dev):
            return send(tok_ref.at[rows, :], tok.at[rows, tcols(xh, y, c)], dev)

        tq["h"] = own(ALL, dev_h)
        tq["pa"], tq["mb"] = own(TA, dev_yp), own(TB, dev_ym)
        tq["pb"], tq["ma"] = own(TB, dev_yp), own(TA, dev_ym)
        tq["c0"] = own(ALL, dev_c)

    def t_partner():
        got(tq["h"])
        tq["hpa"], tq["hmb"] = tsend(oh, y, TA, dev_yp), tsend(oh, y, TB, dev_ym)
        tq["hpb"], tq["hma"] = tsend(oh, y, TB, dev_yp), tsend(oh, y, TA, dev_ym)
        tq["c1"] = tsend(oh, y, ALL, dev_c)

    def t_forward_own():
        got(tq["pa"])
        tq["fa"] = tsend(xh, ym, TA, dev_yp)
        got(tq["mb"])
        tq["fb"] = tsend(xh, yp, TB, dev_ym)
        got(tq["pb"])
        tq["c2"] = tsend(xh, ym, ALL, dev_c)
        got(tq["ma"])
        tq["c3"] = tsend(xh, yp, ALL, dev_c)

    def t_forward_partner():
        got(tq["hpa"])
        tq["hfa"] = tsend(oh, ym, TA, dev_yp)
        got(tq["hmb"])
        tq["hfb"] = tsend(oh, yp, TB, dev_ym)
        got(tq["hpb"])
        tq["c4"] = tsend(oh, ym, ALL, dev_c)
        got(tq["hma"])
        tq["c5"] = tsend(oh, yp, ALL, dev_c)

    def t_last():
        got(tq["fa"], tq["fb"])
        tq["c6"] = tsend(xh, y2, ALL, dev_c)
        got(tq["hfa"], tq["hfb"])
        tq["c7"] = tsend(oh, y2, ALL, dev_c)

    def t_done():
        got(*(tq["c%d" % i] for i in range(8)))

    def hidden(h):
        cols = pl.ds(h * BLK, BLK)

        def tile(i, carry):
            at = pl.ds(pl.multiple_of(i * 256, 256), 256)
            hid[...] = dot(tok[at, :], wf[:, cols])

            def slope(j, inner):
                small = pl.ds(pl.multiple_of(j * 16, 16), 16)
                big = pl.ds(pl.multiple_of(i * 256 + j * 16, 16), 16)
                cot = hg[big, cols].astype(F32)
                hg[big, cols] = (cot * gelu_slope(hid[small, :])).astype(BF16)
                return inner

            lax.fori_loop(0, 16, slope, 0)
            return carry

        lax.fori_loop(0, TOK // 256, tile, 0)

    def gradient(h):
        cols = pl.ds(h * BLK, BLK)
        for i in range(4):
            at = pl.ds(i * 256, 256)
            hgt[:, at] = hg[at, cols].T

        def block(d, carry):
            at = pl.ds(pl.multiple_of(d * BLK, BLK), BLK)
            part[h, d] = (dot(hgt[...], tok[:, at]) * grad_scale).astype(BF16)
            return carry

        lax.fori_loop(0, 8, block, 0)

    def input_part():
        def block(n, carry):
            at = pl.ds(pl.multiple_of(n * BLK, BLK), BLK)
            tok[:, at] = lax.dot_general(
                hg[...], wf[at, :], (((1,), (1,)), ((), ())), preferred_element_type=F32
            ).astype(BF16)
            return carry

        lax.fori_loop(0, 8, block, 0)

    def ppart(h, zi, li, rows):
        return part.at[h, zi * 2 + li, pl.ds(rows[0], rows[1]), :]

    gstate = [dict(), dict()]
    OTHER, OWN = 0, 1
    DN, UP = 0, 1

    def g_start(h):
        q = gstate[h]
        for zi, name in ((u2, "rz2"), (up, "rzp"), (um, "rzm"), (z, "rz0")):
            q[name] = send(ppart(h, zi, m, ZZ), rz.at[h, zi], dev_x)
        for side, li in ((OTHER, m), (OWN, l)):
            q["1p", side] = send(ppart(h, u2, li, XA), s1.at[h, UP, side], dev_zp)
            q["1m", side] = send(ppart(h, u2, li, XB), s1.at[h, DN, side], dev_zm)
        for side, li in ((OTHER, m), (OWN, l)):
            q["2pb", side] = send(ppart(h, up, li, XB), s2.at[h, UP, side, 1], dev_zp)
            q["2ma", side] = send(ppart(h, um, li, XA), s2.at[h, DN, side, 0], dev_zm)

    def g_second(h):
        q = gstate[h]
        for side, li in ((OTHER, m), (OWN, l)):
            got(q["1p", side])
            mine = ppart(h, up, li, XA)
            add_rows(mine, (mine, s1.at[h, UP, side]), XA[1])
            q["2pa", side] = send(mine, s2.at[h, UP, side, 0], dev_zp)
            got(q["1m", side])
            mine = ppart(h, um, li, XB)
            add_rows(mine, (mine, s1.at[h, DN, side]), XB[1])
            q["2mb", side] = send(mine, s2.at[h, DN, side, 1], dev_zm)

    def g_middle(h):
        q = gstate[h]
        for zi, name in ((u2, "rz2"), (up, "rzp"), (um, "rzm"), (z, "rz0")):
            got(q[name])
            mine = ppart(h, zi, l, ZZ)
            add_rows(mine, (mine, rz.at[h, zi]), ZZ[1])
        q["z1p"] = send(ppart(h, u2, l, ZA), s1z.at[h, UP], dev_zp)
        q["z1m"] = send(ppart(h, u2, l, ZB), s1z.at[h, DN], dev_zm)
        q["z2pb"] = send(ppart(h, up, l, ZB), s2z.at[h, UP, 1], dev_zp)
        q["z2ma"] = send(ppart(h, um, l, ZA), s2z.at[h, DN, 0], dev_zm)

    def g_middle_second(h):
        q = gstate[h]
        got(q["z1p"])
        mine = ppart(h, up, l, ZA)
        add_rows(mine, (mine, s1z.at[h, UP]), ZA[1])
        q["z2pa"] = send(mine, s2z.at[h, UP, 0], dev_zp)
        got(q["z1m"])
        mine = ppart(h, um, l, ZB)
        add_rows(mine, (mine, s1z.at[h, DN]), ZB[1])
        q["z2mb"] = send(mine, s2z.at[h, DN, 1], dev_zm)

    def g_cross(h):
        q = gstate[h]
        for k, rows, name in ((0, XA, "a"), (1, XB, "b")):
            got(q["2p" + name, OTHER], q["2m" + name, OTHER])
            mine = ppart(h, z, m, rows)
            add_rows(mine, (mine, s2.at[h, UP, OTHER, k], s2.at[h, DN, OTHER, k]), rows[1])
            q["x" + name] = send(mine, rx.at[h, k], dev_x)

    def g_final(h):
        q = gstate[h]
        for k, rows, name in ((0, ZA, "a"), (1, ZB, "b")):
            got(q["z2p" + name], q["z2m" + name])
            add_rows(
                gt_ref.at[h, pl.ds(rows[0], rows[1]), :],
                (ppart(h, z, l, rows), s2z.at[h, UP, k], s2z.at[h, DN, k]),
                rows[1],
            )
        for k, rows, name in ((0, XA, "a"), (1, XB, "b")):
            got(q["2p" + name, OWN], q["2m" + name, OWN], q["x" + name])
            add_rows(
                gt_ref.at[h, pl.ds(rows[0], rows[1]), :],
                (ppart(h, z, l, rows), s2.at[h, UP, OWN, k], s2.at[h, DN, OWN, k], rx.at[h, k]),
                rows[1],
            )

    dq = {}

    def dpart(hi, yi, ci, rows):
        return tok.at[rows, tcols(hi, yi, ci)]

    sides = ((OTHER, oh), (OWN, xh))

    def d_start():
        for yi, name in ((y2, "2"), (yp, "p"), (ym, "m"), (y, "0")):
            for side, hi in sides:
                dq["c" + name, side] = send(
                    dpart(hi, yi, oc, ALL), sib.at[hi * 4 + yi], dev_c
                )

    def d_add(name, yi):
        for side, hi in sides:
            got(dq["c" + name, side])
            mine = dpart(hi, yi, c, ALL)
            add_rows(mine, (mine, sib.at[hi * 4 + yi]), TOK)

    def d_first():
        d_add("2", y2)
        for side, hi in sides:
            dq["1p", side] = send(dpart(hi, y2, c, TA), t1.at[UP, side], dev_yp)
            dq["1m", side] = send(dpart(hi, y2, c, TB), t1.at[DN, side], dev_ym)
        d_add("p", yp)
        for side, hi in sides:
            dq["2pb", side] = send(dpart(hi, yp, c, TB), t2.at[UP, side, 1], dev_yp)
        d_add("m", ym)
        for side, hi in sides:
            dq["2ma", side] = send(dpart(hi, ym, c, TA), t2.at[DN, side, 0], dev_ym)
        d_add("0", y)

    def d_second():
        for side, hi in sides:
            got(dq["1p", side])
            mine = dpart(hi, yp, c, TA)
            add_rows(mine, (mine, t1.at[UP, side]), TOK // 2)
            dq["2pa", side] = send(mine, t2.at[UP, side, 0], dev_yp)
            got(dq["1m", side])
            mine = dpart(hi, ym, c, TB)
            add_rows(mine, (mine, t1.at[DN, side]), TOK // 2)
            dq["2mb", side] = send(mine, t2.at[DN, side, 1], dev_ym)

    def d_cross():
        for k, rows, name in ((0, TA, "a"), (1, TB, "b")):
            got(dq["2p" + name, OTHER], dq["2m" + name, OTHER])
            mine = dpart(oh, y, c, rows)
            add_rows(mine, (mine, t2.at[UP, OTHER, k], t2.at[DN, OTHER, k]), TOK // 2)
            dq["x" + name] = send(mine, tx.at[k], dev_h)

    def d_final():
        for k, rows, name in ((0, TA, "a"), (1, TB, "b")):
            got(dq["2p" + name, OWN], dq["2m" + name, OWN], dq["x" + name])
            add_rows(
                tg_ref.at[rows, :],
                (dpart(xh, y, c, rows), t2.at[UP, OWN, k], t2.at[DN, OWN, k], tx.at[k]),
                TOK // 2,
            )

    local = [
        pltpu.make_async_copy(w_ref, wf.at[rows_of(z, l, (0, BLK)), :], ls.at[0]),
        pltpu.make_async_copy(tok_ref, tok.at[:, tcols(xh, y, c)], ls.at[1]),
        pltpu.make_async_copy(cot_ref, hg, ls.at[2]),
    ]
    w_own(0)
    t_own()
    for copy in local:
        copy.start()
    t_partner()
    w_partner(0)
    t_forward_own()
    w_forward_own(0)
    t_forward_partner()
    w_forward_partner(0)
    w_own(1)
    t_last()
    w_last(0)
    for copy in local:
        copy.wait()
    t_done()
    w_done(0)
    w_partner(1)
    hidden(0)
    w_forward_own(1)
    gradient(0)
    g_start(0)
    w_forward_partner(1)
    w_last(1)
    g_second(0)
    g_middle(0)
    w_done(1)
    hidden(1)
    g_middle_second(0)
    gradient(1)
    g_start(1)
    g_cross(0)
    for copy in tq.values():
        copy.wait_send()
    input_part()
    d_start()
    g_second(1)
    d_first()
    g_middle(1)
    g_final(0)
    d_second()
    g_middle_second(1)
    d_cross()
    g_cross(1)
    d_final()
    g_final(1)
    waited = [id(copy) for copy in tq.values()]
    for copy in copies:
        if id(copy) not in waited:
            copy.wait_send()


def exchange(tokens, weight, cotangent):
    any_spec = pl.BlockSpec(memory_space=pl.ANY)
    vmem_spec = pl.BlockSpec(memory_space=pltpu.VMEM)
    dma = pltpu.SemaphoreType.DMA
    return pl.pallas_call(
        exchange_kernel,
        out_shape=(
            jax.ShapeDtypeStruct((TOK, FEAT), BF16),
            jax.ShapeDtypeStruct((2, BLK, BLK), F32),
        ),
        in_specs=[any_spec, any_spec, any_spec],
        out_specs=(vmem_spec, vmem_spec),
        scratch_shapes=[
            pltpu.VMEM((D, COLS), BF16),
            pltpu.VMEM((TOK, D), BF16),
            pltpu.VMEM((TOK, COLS), BF16),
            pltpu.VMEM((BLK, TOK), BF16),
            pltpu.VMEM((256, BLK), F32),
            pltpu.VMEM((2, 8, BLK, BLK), BF16),
            pltpu.VMEM((2, 2, 2, XA[1], BLK), BF16),
            pltpu.VMEM((2, 2, ZA[1], BLK), BF16),
            pltpu.VMEM((2, 2, 2, 2, XA[1], BLK), BF16),
            pltpu.VMEM((2, 2, 2, ZA[1], BLK), BF16),
            pltpu.VMEM((2, 4, ZZ[1], BLK), BF16),
            pltpu.VMEM((2, 2, XA[1], BLK), BF16),
            pltpu.VMEM((8, TOK, FEAT), BF16),
            pltpu.VMEM((2, 2, TOK // 2, FEAT), BF16),
            pltpu.VMEM((2, 2, 2, TOK // 2, FEAT), BF16),
            pltpu.VMEM((2, TOK // 2, FEAT), BF16),
            dma((NSEM,)),
            dma((NSEM,)),
            dma((3,)),
        ],
        compiler_params=pltpu.CompilerParams(
            collective_id=0, has_side_effects=True, vmem_limit_bytes=60 * 2**20
        ),
        cost_estimate=pl.CostEstimate(
            flops=6 * TOK * D * COLS, bytes_accessed=2**24, transcendentals=2 * TOK * COLS
        ),
        name="exchange",
    )(tokens, weight, cotangent)


def total_of(values):
    return jnp.sum(jnp.sum(values, axis=1, keepdims=True), axis=0, keepdims=True)


def precondition_kernel(gt_ref, left_ref, right_ref, update_ref, left_out, right_out):
    gt = gt_ref[0]
    grad = gt.T
    gth, gh = gt.astype(BF16), grad.astype(BF16)
    rows = lax.broadcasted_iota(jnp.int32, (BLK, BLK), 0)
    cols = lax.broadcasted_iota(jnp.int32, (BLK, BLK), 1)
    eye = jnp.where(rows == cols, 1.0, 0.0).astype(F32)
    share = (1.0 - decay_rate) / BLK
    left = decay_rate * left_ref[0, 0] + share * dot(gh, gth)
    right = decay_rate * right_ref[0, 0] + share * dot(gth, gh)
    left_out[0, 0] = left
    right_out[0, 0] = right

    def each(function, *lists):
        return [function(*items) for items in zip(*lists)]

    def start(stat):
        trace = total_of(stat * eye)
        regular = stat + (ridge_share * trace / BLK) * eye
        scale = jnp.sqrt(total_of(regular * regular)) / 4.0
        return regular / scale, scale

    begun = each(start, (left, right))
    first = [b[0] for b in begun]
    scales = [b[1] for b in begun]
    firsth = each(lambda a: a.astype(BF16), first)
    square = each(dot, firsth, firsth)
    zero_sq = each(
        lambda a, q: (1.5625 * eye - 0.625 * a + 0.0625 * q).astype(BF16), first, square
    )
    crossed = each(lambda a, q: (1.25 * a - 0.25 * q).astype(BF16), first, square)
    fourth = each(lambda a: dot(a, a).astype(BF16), zero_sq)
    two = each(
        lambda a, f, x: 1.5625 * eye - 0.3125 * a - 0.25 * dot(f, x), first, fourth, crossed
    )
    twoh = each(lambda a: a.astype(BF16), two)
    two_sq = each(lambda a: dot(a, a).astype(BF16), twoh)
    two_crossed = each(lambda a, f: dot(a, f).astype(BF16), twoh, firsth)
    two_fourth = each(lambda a: dot(a, a).astype(BF16), two_sq)
    roots = each(
        lambda a, f, x, s: (
            lax.rsqrt(jnp.sqrt(s)) * (1.25 * a - 0.25 * dot(f, x))
        ).astype(BF16),
        two, two_fourth, two_crossed, scales,
    )
    left_part = dot(roots[0], gh).astype(BF16)
    raw = dot(left_part, roots[1])
    size = float(BLK * BLK)
    grad_rms = jnp.sqrt(total_of(gt * gt) / size)
    raw_rms = jnp.sqrt(total_of(raw * raw) / size + epsilon)
    update_ref[...] = (raw * (grad_rms / raw_rms)).astype(BF16)


def precondition(gt, left_stats, right_stats):
    stat_spec = pl.BlockSpec((1, 1, BLK, BLK), lambda h: (0, h, 0, 0))
    return pl.pallas_call(
        precondition_kernel,
        grid=(2,),
        out_shape=(
            jax.ShapeDtypeStruct((BLK, COLS), BF16),
            jax.ShapeDtypeStruct(left_stats.shape, F32),
            jax.ShapeDtypeStruct(right_stats.shape, F32),
        ),
        in_specs=[pl.BlockSpec((1, BLK, BLK), lambda h: (h, 0, 0)), stat_spec, stat_spec],
        out_specs=(pl.BlockSpec((BLK, BLK), lambda h: (0, h)), stat_spec, stat_spec),
        compiler_params=pltpu.CompilerParams(vmem_limit_bytes=56 * 2**20),
        name="precondition",
    )(gt, left_stats, right_stats)


def shards(tokens, weight, cotangent, left_stats, right_stats):
    tokens_grad, gt = exchange(tokens, weight, cotangent)
    update, left_new, right_new = precondition(gt, left_stats, right_stats)
    return tokens_grad, update, left_new, right_new


def solution(mesh):
    two = P("dp", ("tensor", "pre"))
    four = P("dp", ("tensor", "pre"), None, None)
    return jax.shard_map(
        shards,
        mesh=mesh,
        in_specs=(two, two, two, four, four),
        out_specs=(two, two, four, four),
        check_vma=False,
    )
```

```python
import jax
import jax.numpy as jnp
from jax import lax
from jax.experimental import pallas as pl
from jax.experimental.pallas import tpu as pltpu
from jax.sharding import PartitionSpec as P

MESH = pl.DeviceIdType.MESH
F32 = jnp.float32
BF16 = jnp.bfloat16

TOK = 1024
D = 4096
BLK = 512
COLS = 1024
FEAT = 256

decay_rate = 0.5
ridge_share = 0.05
epsilon = 1e-06
grad_scale = float(8192) ** (-0.5)

XA = (0, 176)
ZA = (176, 80)
ZB = (256, 80)
XB = (336, 176)
ZZ = (176, 160)
HA = (0, 256)
HB = (256, 256)
NSEM = 160


def dot(a, b):
    return jnp.dot(a, b, preferred_element_type=F32)


def gelu_slope(values):
    return (
        0.5 * (1.0 + lax.erf(values * 0.7071067811865476))
        + values * jnp.exp(-0.5 * values * values) * 0.3989422804014327
    )


def add_rows(dst, sources, rows, chunk=16):
    def body(i, carry):
        at = pl.ds(pl.multiple_of(i * chunk, chunk), chunk)
        total = sources[0][at, :].astype(F32)
        for source in sources[1:]:
            total = total + source[at, :].astype(F32)
        dst[at, :] = total.astype(dst.dtype)
        return carry

    lax.fori_loop(0, rows // chunk, body, 0)


def exchange_kernel(
    tok_ref, w_ref, cot_ref, tg_ref, gt_ref,
    wf, tok, hg, hgt, hid, part, dout,
    s1, s1z, s2, s2z, rz, rx, sib, t1, t2, tx,
    ss, rs, ls,
):
    dp = lax.axis_index("dp")
    tn = lax.axis_index("tensor")
    c = lax.axis_index("pre")
    z, l = lax.div(dp, 2), lax.rem(dp, 2)
    xh, y = lax.div(tn, 4), lax.rem(tn, 4)
    m = 1 - l
    up, um, u2 = lax.rem(z + 1, 4), lax.rem(z + 3, 4), lax.rem(z + 2, 4)
    yp, ym, y2 = lax.rem(y + 1, 4), lax.rem(y + 3, 4), lax.rem(y + 2, 4)
    oh, oc = 1 - xh, 1 - c
    dev_zp, dev_zm = (up * 2 + l, tn, c), (um * 2 + l, tn, c)
    dev_x = (z * 2 + m, tn, c)
    dev_yp, dev_ym = (dp, xh * 4 + yp, c), (dp, xh * 4 + ym, c)
    dev_h = (dp, oh * 4 + y, c)
    dev_c = (dp, tn, oc)

    barrier = pltpu.get_barrier_semaphore()
    for dev in (dev_zp, dev_zm, dev_x, dev_yp, dev_ym, dev_h, dev_c):
        pl.semaphore_signal(barrier, inc=1, device_id=dev, device_id_type=MESH)
    pl.semaphore_wait(barrier, 7)

    copies = []

    def send(src, dst, dev):
        k = len(copies)
        copy = pltpu.make_async_remote_copy(
            src_ref=src, dst_ref=dst, send_sem=ss.at[k], recv_sem=rs.at[k],
            device_id=dev, device_id_type=MESH,
        )
        copy.start()
        copies.append(copy)
        return copy

    def got(*several):
        for copy in several:
            copy.wait_recv()

    def rows_of(zi, li, rows):
        return pl.ds(pl.multiple_of((zi * 2 + li) * BLK + rows[0], 16), rows[1])

    def wpart(zi, li, rows, h):
        return wf.at[rows_of(zi, li, rows), pl.ds(h * BLK, BLK)]

    def wsend(zi, li, rows, h, dev):
        ref = wpart(zi, li, rows, h)
        return send(ref, ref, dev)

    wstate = [dict(), dict()]

    def w_own(h, first):
        q = wstate[h]

        def own(rows, dev):
            return send(
                w_ref.at[pl.ds(rows[0], rows[1]), pl.ds(h * BLK, BLK)],
                wpart(z, l, rows, h), dev,
            )

        if first:
            q["pa"], q["mb"] = own(HA, dev_zp), own(HB, dev_zm)
            q["xa"], q["xb"] = own(XA, dev_x), own(XB, dev_x)
        else:
            q["pb"], q["ma"] = own(HB, dev_zp), own(HA, dev_zm)
            q["xz"] = own(ZZ, dev_x)

    def w_partner(h):
        q = wstate[h]
        got(q["xa"])
        q["ppa"] = wsend(z, m, XA, h, dev_zp)
        got(q["xb"])
        q["pmb"] = wsend(z, m, XB, h, dev_zm)
        q["ppb"] = wsend(z, m, XB, h, dev_zp)
        q["pma"] = wsend(z, m, XA, h, dev_zm)

    def w_forward_own(h):
        q = wstate[h]
        got(q["pa"])
        q["fa"] = wsend(um, l, HA, h, dev_zp)
        got(q["mb"])
        q["fb"] = wsend(up, l, HB, h, dev_zm)

    def w_cross(h):
        q = wstate[h]
        got(q["pb"])
        q["xzm"] = wsend(um, l, ZZ, h, dev_x)
        got(q["ma"])
        q["xzp"] = wsend(up, l, ZZ, h, dev_x)

    def w_forward_partner(h):
        q = wstate[h]
        got(q["ppa"])
        q["fpa"] = wsend(um, m, XA, h, dev_zp)
        got(q["pmb"])
        q["fpb"] = wsend(up, m, XB, h, dev_zm)

    def w_last(h):
        q = wstate[h]
        got(q["fa"])
        q["x2a"] = wsend(u2, l, ZA, h, dev_x)
        got(q["fb"])
        q["x2b"] = wsend(u2, l, ZB, h, dev_x)

    def w_done(h):
        q = wstate[h]
        got(*(q[k] for k in ("xz", "ppb", "pma", "xzm", "xzp", "fpa", "fpb", "x2a", "x2b")))

    TA, TB = pl.ds(0, TOK // 2), pl.ds(TOK // 2, TOK // 2)
    ALL = pl.ds(0, TOK)

    def tcols(hi, yi, ci):
        return pl.ds(pl.multiple_of(((hi * 4 + yi) * 2 + ci) * FEAT, FEAT), FEAT)

    def tsend(hi, yi, rows, dev):
        ref = tok.at[rows, tcols(hi, yi, c)]
        return send(ref, ref, dev)

    tq = {}

    def t_own():
        def own(rows, dev):
            return send(tok_ref.at[rows, :], tok.at[rows, tcols(xh, y, c)], dev)

        tq["h"] = own(ALL, dev_h)
        tq["pa"], tq["mb"] = own(TA, dev_yp), own(TB, dev_ym)
        tq["pb"], tq["ma"] = own(TB, dev_yp), own(TA, dev_ym)
        tq["c0"] = own(ALL, dev_c)

    def t_partner():
        got(tq["h"])
        tq["hpa"], tq["hmb"] = tsend(oh, y, TA, dev_yp), tsend(oh, y, TB, dev_ym)
        tq["hpb"], tq["hma"] = tsend(oh, y, TB, dev_yp), tsend(oh, y, TA, dev_ym)
        tq["c1"] = tsend(oh, y, ALL, dev_c)

    def t_forward_own():
        got(tq["pa"])
        tq["fa"] = tsend(xh, ym, TA, dev_yp)
        got(tq["mb"])
        tq["fb"] = tsend(xh, yp, TB, dev_ym)

    def t_share_own():
        got(tq["pb"])
        tq["c2"] = tsend(xh, ym, ALL, dev_c)
        got(tq["ma"])
        tq["c3"] = tsend(xh, yp, ALL, dev_c)

    def t_forward_partner():
        got(tq["hpa"])
        tq["hfa"] = tsend(oh, ym, TA, dev_yp)
        got(tq["hmb"])
        tq["hfb"] = tsend(oh, yp, TB, dev_ym)
        got(tq["hpb"])
        tq["c4"] = tsend(oh, ym, ALL, dev_c)
        got(tq["hma"])
        tq["c5"] = tsend(oh, yp, ALL, dev_c)

    def t_last_own():
        got(tq["fa"], tq["fb"])
        tq["c6"] = tsend(xh, y2, ALL, dev_c)

    def t_last():
        got(tq["hfa"], tq["hfb"])
        tq["c7"] = tsend(oh, y2, ALL, dev_c)

    def t_done():
        got(*(tq["c%d" % i] for i in range(8)))

    dq = {}

    def hidden(h, r):
        cols = pl.ds(h * BLK, BLK)

        def tile(i, carry):
            at = pl.ds(pl.multiple_of(i * 256, 256), 256)
            hid[...] = dot(tok[at, :], wf[:, cols])

            def slope(j, inner):
                small = pl.ds(pl.multiple_of(j * 16, 16), 16)
                big = pl.ds(pl.multiple_of(i * 256 + j * 16, 16), 16)
                cot = hg[big, cols].astype(F32)
                hg[big, cols] = (cot * gelu_slope(hid[small, :])).astype(BF16)
                return inner

            lax.fori_loop(0, 16, slope, 0)
            return carry

        lax.fori_loop(2 * r, 2 * r + 2, tile, 0)

    def gradient(h):
        cols = pl.ds(h * BLK, BLK)
        for i in range(4):
            at = pl.ds(i * 256, 256)
            hgt[:, at] = hg[at, cols].T

        def block(d, carry):
            at = pl.ds(pl.multiple_of(d * BLK, BLK), BLK)
            part[h, d] = (dot(hgt[...], tok[:, at]) * grad_scale).astype(BF16)
            return carry

        lax.fori_loop(0, 8, block, 0)

    def wide_dot(rows, g):
        at = pl.ds(pl.multiple_of(g * FEAT, FEAT), FEAT)
        return lax.dot_general(
            hg[rows, :], wf[at, :], (((1,), (1,)), ((), ())), preferred_element_type=F32
        )

    def input_other(r):
        rows = pl.ds(r * (TOK // 2), TOK // 2)

        def block(t, carry):
            dout[t, rows, :] = wide_dot(rows, t * 2 + oc).astype(BF16)
            return carry

        lax.fori_loop(0, 8, block, 0)
        dq["c", r] = send(dout.at[:, rows, :], sib.at[:, rows, :], dev_c)

    def input_own(r):
        got(dq["c", r])
        rows = pl.ds(r * (TOK // 2), TOK // 2)

        def block(t, carry):
            mine = wide_dot(rows, t * 2 + c) + sib[t, rows, :].astype(F32)
            sib[t, rows, :] = mine.astype(BF16)
            return carry

        lax.fori_loop(0, 8, block, 0)

    def ppart(h, zi, li, rows):
        return part.at[h, zi * 2 + li, pl.ds(rows[0], rows[1]), :]

    gstate = [dict(), dict()]
    OTHER, OWN = 0, 1
    DN, UP = 0, 1

    def g_start(h):
        q = gstate[h]
        for zi, name in ((u2, "rz2"), (up, "rzp"), (um, "rzm"), (z, "rz0")):
            q[name] = send(ppart(h, zi, m, ZZ), rz.at[h, zi], dev_x)
        for side, li in ((OTHER, m), (OWN, l)):
            q["1p", side] = send(ppart(h, u2, li, XA), s1.at[h, UP, side], dev_zp)
            q["1m", side] = send(ppart(h, u2, li, XB), s1.at[h, DN, side], dev_zm)
        for side, li in ((OTHER, m), (OWN, l)):
            q["2pb", side] = send(ppart(h, up, li, XB), s2.at[h, UP, side, 1], dev_zp)
            q["2ma", side] = send(ppart(h, um, li, XA), s2.at[h, DN, side, 0], dev_zm)

    def g_second(h):
        q = gstate[h]
        for side, li in ((OTHER, m), (OWN, l)):
            got(q["1p", side])
            mine = ppart(h, up, li, XA)
            add_rows(mine, (mine, s1.at[h, UP, side]), XA[1])
            q["2pa", side] = send(mine, s2.at[h, UP, side, 0], dev_zp)
            got(q["1m", side])
            mine = ppart(h, um, li, XB)
            add_rows(mine, (mine, s1.at[h, DN, side]), XB[1])
            q["2mb", side] = send(mine, s2.at[h, DN, side, 1], dev_zm)

    def g_middle(h):
        q = gstate[h]
        for zi, name in ((u2, "rz2"), (up, "rzp"), (um, "rzm"), (z, "rz0")):
            got(q[name])
            mine = ppart(h, zi, l, ZZ)
            add_rows(mine, (mine, rz.at[h, zi]), ZZ[1])
        q["z1p"] = send(ppart(h, u2, l, ZA), s1z.at[h, UP], dev_zp)
        q["z1m"] = send(ppart(h, u2, l, ZB), s1z.at[h, DN], dev_zm)
        q["z2pb"] = send(ppart(h, up, l, ZB), s2z.at[h, UP, 1], dev_zp)
        q["z2ma"] = send(ppart(h, um, l, ZA), s2z.at[h, DN, 0], dev_zm)

    def g_middle_second(h):
        q = gstate[h]
        got(q["z1p"])
        mine = ppart(h, up, l, ZA)
        add_rows(mine, (mine, s1z.at[h, UP]), ZA[1])
        q["z2pa"] = send(mine, s2z.at[h, UP, 0], dev_zp)
        got(q["z1m"])
        mine = ppart(h, um, l, ZB)
        add_rows(mine, (mine, s1z.at[h, DN]), ZB[1])
        q["z2mb"] = send(mine, s2z.at[h, DN, 1], dev_zm)

    def g_cross(h):
        q = gstate[h]
        for k, rows, name in ((0, XA, "a"), (1, XB, "b")):
            got(q["2p" + name, OTHER], q["2m" + name, OTHER])
            mine = ppart(h, z, m, rows)
            add_rows(mine, (mine, s2.at[h, UP, OTHER, k], s2.at[h, DN, OTHER, k]), rows[1])
            q["x" + name] = send(mine, rx.at[h, k], dev_x)

    def g_final(h):
        q = gstate[h]
        for k, rows, name in ((0, ZA, "a"), (1, ZB, "b")):
            got(q["z2p" + name], q["z2m" + name])
            add_rows(
                gt_ref.at[h, pl.ds(rows[0], rows[1]), :],
                (ppart(h, z, l, rows), s2z.at[h, UP, k], s2z.at[h, DN, k]),
                rows[1],
            )
        for k, rows, name in ((0, XA, "a"), (1, XB, "b")):
            got(q["2p" + name, OWN], q["2m" + name, OWN], q["x" + name])
            add_rows(
                gt_ref.at[h, pl.ds(rows[0], rows[1]), :],
                (ppart(h, z, l, rows), s2.at[h, UP, OWN, k], s2.at[h, DN, OWN, k], rx.at[h, k]),
                rows[1],
            )

    def dpart(hi, yi, ci, rows):
        return sib.at[hi * 4 + yi, rows, :]

    sides = ((OTHER, oh), (OWN, xh))

    def d_first(r):
        for side, hi in sides:
            if r == 0:
                dq["1p", side] = send(dpart(hi, y2, c, TA), t1.at[UP, side], dev_yp)
                dq["2ma", side] = send(dpart(hi, ym, c, TA), t2.at[DN, side, 0], dev_ym)
            else:
                dq["1m", side] = send(dpart(hi, y2, c, TB), t1.at[DN, side], dev_ym)
                dq["2pb", side] = send(dpart(hi, yp, c, TB), t2.at[UP, side, 1], dev_yp)

    def d_second():
        for side, hi in sides:
            got(dq["1p", side])
            mine = dpart(hi, yp, c, TA)
            add_rows(mine, (mine, t1.at[UP, side]), TOK // 2)
            dq["2pa", side] = send(mine, t2.at[UP, side, 0], dev_yp)
            got(dq["1m", side])
            mine = dpart(hi, ym, c, TB)
            add_rows(mine, (mine, t1.at[DN, side]), TOK // 2)
            dq["2mb", side] = send(mine, t2.at[DN, side, 1], dev_ym)

    def d_cross():
        for k, rows, name in ((0, TA, "a"), (1, TB, "b")):
            got(dq["2p" + name, OTHER], dq["2m" + name, OTHER])
            mine = dpart(oh, y, c, rows)
            add_rows(mine, (mine, t2.at[UP, OTHER, k], t2.at[DN, OTHER, k]), TOK // 2)
            dq["x" + name] = send(mine, tx.at[k], dev_h)

    def d_final():
        for k, rows, name in ((0, TA, "a"), (1, TB, "b")):
            got(dq["2p" + name, OWN], dq["2m" + name, OWN], dq["x" + name])
            add_rows(
                tg_ref.at[rows, :],
                (dpart(xh, y, c, rows), t2.at[UP, OWN, k], t2.at[DN, OWN, k], tx.at[k]),
                TOK // 2,
            )

    local = [
        pltpu.make_async_copy(w_ref, wf.at[rows_of(z, l, (0, BLK)), :], ls.at[0]),
        pltpu.make_async_copy(tok_ref, tok.at[:, tcols(xh, y, c)], ls.at[1]),
        pltpu.make_async_copy(cot_ref, hg, ls.at[2]),
    ]
    w_own(0, True)
    w_own(0, False)
    t_own()
    t_forward_own()
    for copy in local:
        copy.start()
    w_forward_own(0)
    w_own(1, True)
    w_last(0)
    w_partner(0)
    w_cross(0)
    t_partner()
    w_own(1, False)
    w_forward_partner(0)
    w_forward_own(1)
    t_last_own()
    w_partner(1)
    t_forward_partner()
    t_share_own()
    w_cross(1)
    w_done(0)
    t_last()
    t_done()
    for copy in local:
        copy.wait()
    hidden(0, 1)
    hidden(0, 0)
    w_forward_partner(1)
    w_last(1)
    gradient(0)
    g_start(0)
    w_done(1)
    hidden(1, 0)
    hidden(1, 1)
    input_other(0)
    g_second(0)
    gradient(1)
    input_own(0)
    d_first(0)
    g_start(1)
    input_other(1)
    input_own(1)
    g_cross(0)
    d_first(1)
    g_second(1)
    d_second()
    g_cross(1)
    g_middle(0)
    g_middle_second(0)
    d_cross()
    g_middle(1)
    g_final(0)
    g_middle_second(1)
    g_final(1)
    d_final()
    for copy in copies:
        copy.wait_send()


def exchange(tokens, weight, cotangent):
    any_spec = pl.BlockSpec(memory_space=pl.ANY)
    vmem_spec = pl.BlockSpec(memory_space=pltpu.VMEM)
    dma = pltpu.SemaphoreType.DMA
    return pl.pallas_call(
        exchange_kernel,
        out_shape=(
            jax.ShapeDtypeStruct((TOK, FEAT), BF16),
            jax.ShapeDtypeStruct((2, BLK, BLK), F32),
        ),
        in_specs=[any_spec, any_spec, any_spec],
        out_specs=(vmem_spec, vmem_spec),
        scratch_shapes=[
            pltpu.VMEM((D, COLS), BF16),
            pltpu.VMEM((TOK, D), BF16),
            pltpu.VMEM((TOK, COLS), BF16),
            pltpu.VMEM((BLK, TOK), BF16),
            pltpu.VMEM((256, BLK), F32),
            pltpu.VMEM((2, 8, BLK, BLK), BF16),
            pltpu.VMEM((8, TOK, FEAT), BF16),
            pltpu.VMEM((2, 2, 2, XA[1], BLK), BF16),
            pltpu.VMEM((2, 2, ZA[1], BLK), BF16),
            pltpu.VMEM((2, 2, 2, 2, XA[1], BLK), BF16),
            pltpu.VMEM((2, 2, 2, ZA[1], BLK), BF16),
            pltpu.VMEM((2, 4, ZZ[1], BLK), BF16),
            pltpu.VMEM((2, 2, XA[1], BLK), BF16),
            pltpu.VMEM((8, TOK, FEAT), BF16),
            pltpu.VMEM((2, 2, TOK // 2, FEAT), BF16),
            pltpu.VMEM((2, 2, 2, TOK // 2, FEAT), BF16),
            pltpu.VMEM((2, TOK // 2, FEAT), BF16),
            dma((NSEM,)),
            dma((NSEM,)),
            dma((3,)),
        ],
        compiler_params=pltpu.CompilerParams(
            collective_id=0, has_side_effects=True, vmem_limit_bytes=60 * 2**20
        ),
        cost_estimate=pl.CostEstimate(
            flops=6 * TOK * D * COLS, bytes_accessed=2**24, transcendentals=2 * TOK * COLS
        ),
        name="exchange",
    )(tokens, weight, cotangent)


def total_of(values):
    return jnp.sum(jnp.sum(values, axis=1, keepdims=True), axis=0, keepdims=True)


def precondition_kernel(gt_ref, left_ref, right_ref, update_ref, left_out, right_out):
    gt = gt_ref[0]
    grad = gt.T
    gth, gh = gt.astype(BF16), grad.astype(BF16)
    rows = lax.broadcasted_iota(jnp.int32, (BLK, BLK), 0)
    cols = lax.broadcasted_iota(jnp.int32, (BLK, BLK), 1)
    eye = jnp.where(rows == cols, 1.0, 0.0).astype(F32)
    share = (1.0 - decay_rate) / BLK
    left = decay_rate * left_ref[0, 0] + share * dot(gh, gth)
    right = decay_rate * right_ref[0, 0] + share * dot(gth, gh)
    left_out[0, 0] = left
    right_out[0, 0] = right

    def each(function, *lists):
        return [function(*items) for items in zip(*lists)]

    def start(stat):
        trace = total_of(stat * eye)
        regular = stat + (ridge_share * trace / BLK) * eye
        scale = jnp.sqrt(total_of(regular * regular)) / 4.0
        return regular / scale, scale

    begun = each(start, (left, right))
    first = [b[0] for b in begun]
    scales = [b[1] for b in begun]
    firsth = each(lambda a: a.astype(BF16), first)
    square = each(dot, firsth, firsth)
    zero_sq = each(
        lambda a, q: (1.5625 * eye - 0.625 * a + 0.0625 * q).astype(BF16), first, square
    )
    crossed = each(lambda a, q: (1.25 * a - 0.25 * q).astype(BF16), first, square)
    fourth = each(lambda a: dot(a, a).astype(BF16), zero_sq)
    two = each(
        lambda a, f, x: 1.5625 * eye - 0.3125 * a - 0.25 * dot(f, x), first, fourth, crossed
    )
    twoh = each(lambda a: a.astype(BF16), two)
    two_sq = each(lambda a: dot(a, a).astype(BF16), twoh)
    two_crossed = each(lambda a, f: dot(a, f).astype(BF16), twoh, firsth)
    two_fourth = each(lambda a: dot(a, a).astype(BF16), two_sq)
    roots = each(
        lambda a, f, x, s: (
            lax.rsqrt(jnp.sqrt(s)) * (1.25 * a - 0.25 * dot(f, x))
        ).astype(BF16),
        two, two_fourth, two_crossed, scales,
    )
    left_part = dot(roots[0], gh).astype(BF16)
    raw = dot(left_part, roots[1])
    size = float(BLK * BLK)
    grad_rms = jnp.sqrt(total_of(gt * gt) / size)
    raw_rms = jnp.sqrt(total_of(raw * raw) / size + epsilon)
    update_ref[...] = (raw * (grad_rms / raw_rms)).astype(BF16)


def precondition(gt, left_stats, right_stats):
    stat_spec = pl.BlockSpec((1, 1, BLK, BLK), lambda h: (0, h, 0, 0))
    return pl.pallas_call(
        precondition_kernel,
        grid=(2,),
        out_shape=(
            jax.ShapeDtypeStruct((BLK, COLS), BF16),
            jax.ShapeDtypeStruct(left_stats.shape, F32),
            jax.ShapeDtypeStruct(right_stats.shape, F32),
        ),
        in_specs=[pl.BlockSpec((1, BLK, BLK), lambda h: (h, 0, 0)), stat_spec, stat_spec],
        out_specs=(pl.BlockSpec((BLK, BLK), lambda h: (0, h)), stat_spec, stat_spec),
        compiler_params=pltpu.CompilerParams(vmem_limit_bytes=56 * 2**20),
        name="precondition",
    )(gt, left_stats, right_stats)


def shards(tokens, weight, cotangent, left_stats, right_stats):
    tokens_grad, gt = exchange(tokens, weight, cotangent)
    update, left_new, right_new = precondition(gt, left_stats, right_stats)
    return tokens_grad, update, left_new, right_new


def solution(mesh):
    two = P("dp", ("tensor", "pre"))
    four = P("dp", ("tensor", "pre"), None, None)
    return jax.shard_map(
        shards,
        mesh=mesh,
        in_specs=(two, two, two, four, four),
        out_specs=(two, two, four, four),
        check_vma=False,
    )
```

```python
import jax
import jax.numpy as jnp
from jax import lax
from jax.experimental import pallas as pl
from jax.experimental.pallas import tpu as pltpu
from jax.sharding import PartitionSpec as P

MESH = pl.DeviceIdType.MESH
F32 = jnp.float32
BF16 = jnp.bfloat16

TOK = 1024
D = 4096
BLK = 512
COLS = 1024
FEAT = 256

decay_rate = 0.5
ridge_share = 0.05
epsilon = 1e-06
grad_scale = float(8192) ** (-0.5)

XA = (0, 176)
ZA = (176, 80)
ZB = (256, 80)
XB = (336, 176)
ZZ = (176, 160)
HA = (0, 256)
HB = (256, 256)
NSEM = 160


def dot(a, b):
    return jnp.dot(a, b, preferred_element_type=F32)


def gelu_slope(values):
    return (
        0.5 * (1.0 + lax.erf(values * 0.7071067811865476))
        + values * jnp.exp(-0.5 * values * values) * 0.3989422804014327
    )


def add_rows(dst, sources, rows, chunk=16):
    def body(i, carry):
        at = pl.ds(pl.multiple_of(i * chunk, chunk), chunk)
        total = sources[0][at, :].astype(F32)
        for source in sources[1:]:
            total = total + source[at, :].astype(F32)
        dst[at, :] = total.astype(dst.dtype)
        return carry

    lax.fori_loop(0, rows // chunk, body, 0)


def total_of(values):
    return jnp.sum(jnp.sum(values, axis=1, keepdims=True), axis=0, keepdims=True)


def exchange_kernel(
    tok_ref, w_ref, cot_ref, left_ref, right_ref, tg_ref, gt_ref, up_ref, lnew_ref, rnew_ref,
    wf, tok, hg, hgt, hid, part, dout,
    s1, s1z, s2, s2z, rz, rx, sib, t1, t2, tx, gt0, stat, work,
    ss, rs, ls,
):
    dp = lax.axis_index("dp")
    tn = lax.axis_index("tensor")
    c = lax.axis_index("pre")
    z, l = lax.div(dp, 2), lax.rem(dp, 2)
    xh, y = lax.div(tn, 4), lax.rem(tn, 4)
    m = 1 - l
    up, um, u2 = lax.rem(z + 1, 4), lax.rem(z + 3, 4), lax.rem(z + 2, 4)
    yp, ym, y2 = lax.rem(y + 1, 4), lax.rem(y + 3, 4), lax.rem(y + 2, 4)
    oh, oc = 1 - xh, 1 - c
    dev_zp, dev_zm = (up * 2 + l, tn, c), (um * 2 + l, tn, c)
    dev_x = (z * 2 + m, tn, c)
    dev_yp, dev_ym = (dp, xh * 4 + yp, c), (dp, xh * 4 + ym, c)
    dev_h = (dp, oh * 4 + y, c)
    dev_c = (dp, tn, oc)

    barrier = pltpu.get_barrier_semaphore()
    for dev in (dev_zp, dev_zm, dev_x, dev_yp, dev_ym, dev_h, dev_c):
        pl.semaphore_signal(barrier, inc=1, device_id=dev, device_id_type=MESH)
    pl.semaphore_wait(barrier, 7)

    copies = []

    def send(src, dst, dev):
        k = len(copies)
        copy = pltpu.make_async_remote_copy(
            src_ref=src, dst_ref=dst, send_sem=ss.at[k], recv_sem=rs.at[k],
            device_id=dev, device_id_type=MESH,
        )
        copy.start()
        copies.append(copy)
        return copy

    def got(*several):
        for copy in several:
            copy.wait_recv()

    def rows_of(zi, li, rows):
        return pl.ds(pl.multiple_of((zi * 2 + li) * BLK + rows[0], 16), rows[1])

    def wpart(zi, li, rows, h):
        return wf.at[rows_of(zi, li, rows), pl.ds(h * BLK, BLK)]

    def wsend(zi, li, rows, h, dev):
        ref = wpart(zi, li, rows, h)
        return send(ref, ref, dev)

    wstate = [dict(), dict()]

    def w_own(h, first):
        q = wstate[h]

        def own(rows, dev):
            return send(
                w_ref.at[pl.ds(rows[0], rows[1]), pl.ds(h * BLK, BLK)],
                wpart(z, l, rows, h), dev,
            )

        if first:
            q["pa"], q["mb"] = own(HA, dev_zp), own(HB, dev_zm)
            q["xa"], q["xb"] = own(XA, dev_x), own(XB, dev_x)
        else:
            q["pb"], q["ma"] = own(HB, dev_zp), own(HA, dev_zm)
            q["xz"] = own(ZZ, dev_x)

    def w_partner(h):
        q = wstate[h]
        got(q["xa"])
        q["ppa"] = wsend(z, m, XA, h, dev_zp)
        got(q["xb"])
        q["pmb"] = wsend(z, m, XB, h, dev_zm)
        q["ppb"] = wsend(z, m, XB, h, dev_zp)
        q["pma"] = wsend(z, m, XA, h, dev_zm)

    def w_forward_own(h):
        q = wstate[h]
        got(q["pa"])
        q["fa"] = wsend(um, l, HA, h, dev_zp)
        got(q["mb"])
        q["fb"] = wsend(up, l, HB, h, dev_zm)

    def w_cross(h):
        q = wstate[h]
        got(q["pb"])
        q["xzm"] = wsend(um, l, ZZ, h, dev_x)
        got(q["ma"])
        q["xzp"] = wsend(up, l, ZZ, h, dev_x)

    def w_forward_partner(h):
        q = wstate[h]
        got(q["ppa"])
        q["fpa"] = wsend(um, m, XA, h, dev_zp)
        got(q["pmb"])
        q["fpb"] = wsend(up, m, XB, h, dev_zm)

    def w_last(h):
        q = wstate[h]
        got(q["fa"])
        q["x2a"] = wsend(u2, l, ZA, h, dev_x)
        got(q["fb"])
        q["x2b"] = wsend(u2, l, ZB, h, dev_x)

    def w_done(h):
        q = wstate[h]
        got(*(q[k] for k in ("xz", "ppb", "pma", "xzm", "xzp", "fpa", "fpb", "x2a", "x2b")))

    TA, TB = pl.ds(0, TOK // 2), pl.ds(TOK // 2, TOK // 2)
    ALL = pl.ds(0, TOK)

    def tcols(hi, yi, ci):
        return pl.ds(pl.multiple_of(((hi * 4 + yi) * 2 + ci) * FEAT, FEAT), FEAT)

    def tsend(hi, yi, rows, dev):
        ref = tok.at[rows, tcols(hi, yi, c)]
        return send(ref, ref, dev)

    tq = {}

    def t_own():
        def own(rows, dev):
            return send(tok_ref.at[rows, :], tok.at[rows, tcols(xh, y, c)], dev)

        tq["h"] = own(ALL, dev_h)
        tq["pa"], tq["mb"] = own(TA, dev_yp), own(TB, dev_ym)
        tq["pb"], tq["ma"] = own(TB, dev_yp), own(TA, dev_ym)
        tq["c0"] = own(ALL, dev_c)

    def t_partner():
        got(tq["h"])
        tq["hpa"], tq["hmb"] = tsend(oh, y, TA, dev_yp), tsend(oh, y, TB, dev_ym)
        tq["hpb"], tq["hma"] = tsend(oh, y, TB, dev_yp), tsend(oh, y, TA, dev_ym)
        tq["c1"] = tsend(oh, y, ALL, dev_c)

    def t_forward_own():
        got(tq["pa"])
        tq["fa"] = tsend(xh, ym, TA, dev_yp)
        got(tq["mb"])
        tq["fb"] = tsend(xh, yp, TB, dev_ym)

    def t_share_own():
        got(tq["pb"])
        tq["c2"] = tsend(xh, ym, ALL, dev_c)
        got(tq["ma"])
        tq["c3"] = tsend(xh, yp, ALL, dev_c)

    def t_forward_partner():
        got(tq["hpa"])
        tq["hfa"] = tsend(oh, ym, TA, dev_yp)
        got(tq["hmb"])
        tq["hfb"] = tsend(oh, yp, TB, dev_ym)
        got(tq["hpb"])
        tq["c4"] = tsend(oh, ym, ALL, dev_c)
        got(tq["hma"])
        tq["c5"] = tsend(oh, yp, ALL, dev_c)

    def t_last_own():
        got(tq["fa"], tq["fb"])
        tq["c6"] = tsend(xh, y2, ALL, dev_c)

    def t_last():
        got(tq["hfa"], tq["hfb"])
        tq["c7"] = tsend(oh, y2, ALL, dev_c)

    def t_done():
        got(*(tq["c%d" % i] for i in range(8)))

    dq = {}

    def hidden(h, r):
        cols = pl.ds(h * BLK, BLK)

        def tile(i, carry):
            at = pl.ds(pl.multiple_of(i * 256, 256), 256)
            hid[...] = dot(tok[at, :], wf[:, cols])

            def slope(j, inner):
                small = pl.ds(pl.multiple_of(j * 16, 16), 16)
                big = pl.ds(pl.multiple_of(i * 256 + j * 16, 16), 16)
                cot = hg[big, cols].astype(F32)
                hg[big, cols] = (cot * gelu_slope(hid[small, :])).astype(BF16)
                return inner

            lax.fori_loop(0, 16, slope, 0)
            return carry

        lax.fori_loop(2 * r, 2 * r + 2, tile, 0)

    def gradient(h):
        cols = pl.ds(h * BLK, BLK)
        for i in range(4):
            at = pl.ds(i * 256, 256)
            hgt[:, at] = hg[at, cols].T

        def block(d, carry):
            at = pl.ds(pl.multiple_of(d * BLK, BLK), BLK)
            part[h, d] = (dot(hgt[...], tok[:, at]) * grad_scale).astype(BF16)
            return carry

        lax.fori_loop(0, 8, block, 0)

    def wide_dot(rows, g):
        at = pl.ds(pl.multiple_of(g * FEAT, FEAT), FEAT)
        return lax.dot_general(
            hg[rows, :], wf[at, :], (((1,), (1,)), ((), ())), preferred_element_type=F32
        )

    def input_other(r):
        rows = pl.ds(r * (TOK // 2), TOK // 2)

        def block(t, carry):
            dout[t, rows, :] = wide_dot(rows, t * 2 + oc).astype(BF16)
            return carry

        lax.fori_loop(0, 8, block, 0)
        dq["c", r] = send(dout.at[:, rows, :], sib.at[:, rows, :], dev_c)

    def input_own(r):
        got(dq["c", r])
        rows = pl.ds(r * (TOK // 2), TOK // 2)

        def block(t, carry):
            mine = wide_dot(rows, t * 2 + c) + sib[t, rows, :].astype(F32)
            sib[t, rows, :] = mine.astype(BF16)
            return carry

        lax.fori_loop(0, 8, block, 0)

    def ppart(h, zi, li, rows):
        return part.at[h, zi * 2 + li, pl.ds(rows[0], rows[1]), :]

    gstate = [dict(), dict()]
    OTHER, OWN = 0, 1
    DN, UP = 0, 1

    def g_start(h):
        q = gstate[h]
        for zi, name in ((u2, "rz2"), (up, "rzp"), (um, "rzm"), (z, "rz0")):
            q[name] = send(ppart(h, zi, m, ZZ), rz.at[h, zi], dev_x)
        for side, li in ((OTHER, m), (OWN, l)):
            q["1p", side] = send(ppart(h, u2, li, XA), s1.at[h, UP, side], dev_zp)
            q["1m", side] = send(ppart(h, u2, li, XB), s1.at[h, DN, side], dev_zm)
        for side, li in ((OTHER, m), (OWN, l)):
            q["2pb", side] = send(ppart(h, up, li, XB), s2.at[h, UP, side, 1], dev_zp)
            q["2ma", side] = send(ppart(h, um, li, XA), s2.at[h, DN, side, 0], dev_zm)

    def g_second(h):
        q = gstate[h]
        for side, li in ((OTHER, m), (OWN, l)):
            got(q["1p", side])
            mine = ppart(h, up, li, XA)
            add_rows(mine, (mine, s1.at[h, UP, side]), XA[1])
            q["2pa", side] = send(mine, s2.at[h, UP, side, 0], dev_zp)
            got(q["1m", side])
            mine = ppart(h, um, li, XB)
            add_rows(mine, (mine, s1.at[h, DN, side]), XB[1])
            q["2mb", side] = send(mine, s2.at[h, DN, side, 1], dev_zm)

    def g_middle(h):
        q = gstate[h]
        for zi, name in ((u2, "rz2"), (up, "rzp"), (um, "rzm"), (z, "rz0")):
            got(q[name])
            mine = ppart(h, zi, l, ZZ)
            add_rows(mine, (mine, rz.at[h, zi]), ZZ[1])
        q["z1p"] = send(ppart(h, u2, l, ZA), s1z.at[h, UP], dev_zp)
        q["z1m"] = send(ppart(h, u2, l, ZB), s1z.at[h, DN], dev_zm)
        q["z2pb"] = send(ppart(h, up, l, ZB), s2z.at[h, UP, 1], dev_zp)
        q["z2ma"] = send(ppart(h, um, l, ZA), s2z.at[h, DN, 0], dev_zm)

    def g_middle_second(h):
        q = gstate[h]
        got(q["z1p"])
        mine = ppart(h, up, l, ZA)
        add_rows(mine, (mine, s1z.at[h, UP]), ZA[1])
        q["z2pa"] = send(mine, s2z.at[h, UP, 0], dev_zp)
        got(q["z1m"])
        mine = ppart(h, um, l, ZB)
        add_rows(mine, (mine, s1z.at[h, DN]), ZB[1])
        q["z2mb"] = send(mine, s2z.at[h, DN, 1], dev_zm)

    def g_cross(h):
        q = gstate[h]
        for k, rows, name in ((0, XA, "a"), (1, XB, "b")):
            got(q["2p" + name, OTHER], q["2m" + name, OTHER])
            mine = ppart(h, z, m, rows)
            add_rows(mine, (mine, s2.at[h, UP, OTHER, k], s2.at[h, DN, OTHER, k]), rows[1])
            q["x" + name] = send(mine, rx.at[h, k], dev_x)

    def g_final(h):
        q = gstate[h]
        out = gt0 if h == 0 else gt_ref
        for k, rows, name in ((0, ZA, "a"), (1, ZB, "b")):
            got(q["z2p" + name], q["z2m" + name])
            add_rows(
                out.at[pl.ds(rows[0], rows[1]), :],
                (ppart(h, z, l, rows), s2z.at[h, UP, k], s2z.at[h, DN, k]),
                rows[1],
            )
        for k, rows, name in ((0, XA, "a"), (1, XB, "b")):
            got(q["2p" + name, OWN], q["2m" + name, OWN], q["x" + name])
            add_rows(
                out.at[pl.ds(rows[0], rows[1]), :],
                (ppart(h, z, l, rows), s2.at[h, UP, OWN, k], s2.at[h, DN, OWN, k], rx.at[h, k]),
                rows[1],
            )

    def dpart(hi, yi, ci, rows):
        return sib.at[hi * 4 + yi, rows, :]

    sides = ((OTHER, oh), (OWN, xh))

    def d_first(r):
        for side, hi in sides:
            if r == 0:
                dq["1p", side] = send(dpart(hi, y2, c, TA), t1.at[UP, side], dev_yp)
                dq["2ma", side] = send(dpart(hi, ym, c, TA), t2.at[DN, side, 0], dev_ym)
            else:
                dq["1m", side] = send(dpart(hi, y2, c, TB), t1.at[DN, side], dev_ym)
                dq["2pb", side] = send(dpart(hi, yp, c, TB), t2.at[UP, side, 1], dev_yp)

    def d_second():
        for side, hi in sides:
            got(dq["1p", side])
            mine = dpart(hi, yp, c, TA)
            add_rows(mine, (mine, t1.at[UP, side]), TOK // 2)
            dq["2pa", side] = send(mine, t2.at[UP, side, 0], dev_yp)
            got(dq["1m", side])
            mine = dpart(hi, ym, c, TB)
            add_rows(mine, (mine, t1.at[DN, side]), TOK // 2)
            dq["2mb", side] = send(mine, t2.at[DN, side, 1], dev_ym)

    def d_cross():
        for k, rows, name in ((0, TA, "a"), (1, TB, "b")):
            got(dq["2p" + name, OTHER], dq["2m" + name, OTHER])
            mine = dpart(oh, y, c, rows)
            add_rows(mine, (mine, t2.at[UP, OTHER, k], t2.at[DN, OTHER, k]), TOK // 2)
            dq["x" + name] = send(mine, tx.at[k], dev_h)

    def d_final():
        for k, rows, name in ((0, TA, "a"), (1, TB, "b")):
            got(dq["2p" + name, OWN], dq["2m" + name, OWN], dq["x" + name])
            add_rows(
                tg_ref.at[rows, :],
                (dpart(xh, y, c, rows), t2.at[UP, OWN, k], t2.at[DN, OWN, k], tx.at[k]),
                TOK // 2,
            )

    def newton(h):
        early = [copy for q in (*wstate, tq) for copy in q.values()]
        for copy in early:
            copy.wait_send()
        released.extend(early)
        for copy in held:
            copy.wait()

        slots = iter(
            [wf.at[pl.ds(i * BLK, BLK), pl.ds(j * BLK, BLK)] for i in range(8) for j in range(2)]
            + [tok.at[pl.ds(0, BLK), pl.ds(j * BLK, BLK)] for j in range(8)]
        )
        gh, gth, lp = next(slots), next(slots), next(slots)
        mh, zs, cr, fo, tw, tq2, tc, tf, root = [(next(slots), next(slots)) for _ in range(9)]
        pieces = [pl.ds(i * 256, 256) for i in range(2)]
        ids = lax.broadcasted_iota(jnp.int32, (256, BLK), 0)
        across = lax.broadcasted_iota(jnp.int32, (256, BLK), 1)
        eyes = [jnp.where(ids + i * 256 == across, 1.0, 0.0).astype(F32) for i in range(2)]
        share = (1.0 - decay_rate) / BLK

        gth[...] = gt0[...].astype(BF16)
        gh[...] = gt0[...].T.astype(BF16)
        trace, norm = [0.0, 0.0], [0.0, 0.0]
        for i, rows in enumerate(pieces):
            for side, (a, b) in enumerate(((gh, gth), (gth, gh))):
                new = decay_rate * stat[side, rows, :] + share * dot(a[rows, :], b[...])
                stat[side, rows, :] = new
                trace[side] += total_of(new * eyes[i])
                norm[side] += total_of(new * new)
        for side, out in enumerate((lnew_ref, rnew_ref)):
            back = pltpu.make_async_copy(stat.at[side], out, ls.at[5 + side])
            back.start()
            backs.append(back)
        scale = [None, None]
        for side in range(2):
            ridge = ridge_share * trace[side] / BLK
            full = norm[side] + 2.0 * ridge * trace[side] + BLK * ridge * ridge
            scale[side] = jnp.sqrt(full) / 4.0
            for i, rows in enumerate(pieces):
                first = (stat[side, rows, :] + ridge * eyes[i]) / scale[side]
                work[side, rows, :] = first
                mh[side][rows, :] = first.astype(BF16)
        for i, rows in enumerate(pieces):
            for side in range(2):
                first = work[side, rows, :]
                square = dot(mh[side][rows, :], mh[side][...])
                zs[side][rows, :] = (1.5625 * eyes[i] - 0.625 * first + 0.0625 * square).astype(BF16)
                cr[side][rows, :] = (1.25 * first - 0.25 * square).astype(BF16)
        for rows in pieces:
            for side in range(2):
                fo[side][rows, :] = dot(zs[side][rows, :], zs[side][...]).astype(BF16)
        for i, rows in enumerate(pieces):
            for side in range(2):
                two = (
                    1.5625 * eyes[i]
                    - 0.3125 * work[side, rows, :]
                    - 0.25 * dot(fo[side][rows, :], cr[side][...])
                )
                work[side, rows, :] = two
                tw[side][rows, :] = two.astype(BF16)
        for rows in pieces:
            for side in range(2):
                tq2[side][rows, :] = dot(tw[side][rows, :], tw[side][...]).astype(BF16)
                tc[side][rows, :] = dot(tw[side][rows, :], mh[side][...]).astype(BF16)
        for rows in pieces:
            for side in range(2):
                tf[side][rows, :] = dot(tq2[side][rows, :], tq2[side][...]).astype(BF16)
        for rows in pieces:
            for side in range(2):
                three = 1.25 * work[side, rows, :] - 0.25 * dot(tf[side][rows, :], tc[side][...])
                root[side][rows, :] = (lax.rsqrt(jnp.sqrt(scale[side])) * three).astype(BF16)
        for rows in pieces:
            lp[rows, :] = dot(root[0][rows, :], gh[...]).astype(BF16)
        raw_sum, grad_sum = 0.0, 0.0
        for rows in pieces:
            raw = dot(lp[rows, :], root[1][...])
            work[0, rows, :] = raw
            raw_sum += total_of(raw * raw)
            grad_sum += total_of(gt0[rows, :] * gt0[rows, :])
        size = float(BLK * BLK)
        ratio = jnp.sqrt(grad_sum / size) / jnp.sqrt(raw_sum / size + epsilon)
        for rows in pieces:
            up_ref[rows, :] = (work[0, rows, :] * ratio).astype(BF16)

    local = [
        pltpu.make_async_copy(w_ref, wf.at[rows_of(z, l, (0, BLK)), :], ls.at[0]),
        pltpu.make_async_copy(tok_ref, tok.at[:, tcols(xh, y, c)], ls.at[1]),
        pltpu.make_async_copy(cot_ref, hg, ls.at[2]),
    ]
    held = [
        pltpu.make_async_copy(left_ref.at[0, 0], stat.at[0], ls.at[3]),
        pltpu.make_async_copy(right_ref.at[0, 0], stat.at[1], ls.at[4]),
    ]
    backs, released = [], []
    w_own(0, True)
    w_own(0, False)
    t_own()
    t_forward_own()
    for copy in local + held:
        copy.start()
    w_forward_own(0)
    w_own(1, True)
    w_last(0)
    w_partner(0)
    w_cross(0)
    t_share_own()
    t_last_own()
    t_partner()
    w_own(1, False)
    w_forward_partner(0)
    w_forward_own(1)
    w_partner(1)
    t_forward_partner()
    w_cross(1)
    w_done(0)
    t_last()
    t_done()
    for copy in local:
        copy.wait()
    hidden(0, 1)
    hidden(0, 0)
    w_forward_partner(1)
    w_last(1)
    gradient(0)
    g_start(0)
    w_done(1)
    hidden(1, 1)
    hidden(1, 0)
    input_other(0)
    g_second(0)
    gradient(1)
    input_own(0)
    d_first(0)
    g_start(1)
    input_other(1)
    input_own(1)
    d_first(1)
    g_cross(0)
    g_second(1)
    d_second()
    g_cross(1)
    g_middle(0)
    g_middle_second(0)
    d_cross()
    g_middle(1)
    g_final(0)
    g_middle_second(1)
    newton(0)
    g_final(1)
    d_final()
    for copy in backs:
        copy.wait()
    for copy in copies:
        if not any(copy is other for other in released):
            copy.wait_send()


def exchange(tokens, weight, cotangent, left_stats, right_stats):
    any_spec = pl.BlockSpec(memory_space=pl.ANY)
    vmem_spec = pl.BlockSpec(memory_space=pltpu.VMEM)
    dma = pltpu.SemaphoreType.DMA
    square = jax.ShapeDtypeStruct((BLK, BLK), F32)
    return pl.pallas_call(
        exchange_kernel,
        out_shape=(
            jax.ShapeDtypeStruct((TOK, FEAT), BF16),
            square,
            jax.ShapeDtypeStruct((BLK, BLK), BF16),
            square,
            square,
        ),
        in_specs=[any_spec] * 5,
        out_specs=(vmem_spec, vmem_spec, vmem_spec, any_spec, any_spec),
        scratch_shapes=[
            pltpu.VMEM((D, COLS), BF16),
            pltpu.VMEM((TOK, D), BF16),
            pltpu.VMEM((TOK, COLS), BF16),
            pltpu.VMEM((BLK, TOK), BF16),
            pltpu.VMEM((256, BLK), F32),
            pltpu.VMEM((2, 8, BLK, BLK), BF16),
            pltpu.VMEM((8, TOK, FEAT), BF16),
            pltpu.VMEM((2, 2, 2, XA[1], BLK), BF16),
            pltpu.VMEM((2, 2, ZA[1], BLK), BF16),
            pltpu.VMEM((2, 2, 2, 2, XA[1], BLK), BF16),
            pltpu.VMEM((2, 2, 2, ZA[1], BLK), BF16),
            pltpu.VMEM((2, 4, ZZ[1], BLK), BF16),
            pltpu.VMEM((2, 2, XA[1], BLK), BF16),
            pltpu.VMEM((8, TOK, FEAT), BF16),
            pltpu.VMEM((2, 2, TOK // 2, FEAT), BF16),
            pltpu.VMEM((2, 2, 2, TOK // 2, FEAT), BF16),
            pltpu.VMEM((2, TOK // 2, FEAT), BF16),
            pltpu.VMEM((BLK, BLK), F32),
            pltpu.VMEM((2, BLK, BLK), F32),
            pltpu.VMEM((2, BLK, BLK), F32),
            dma((NSEM,)),
            dma((NSEM,)),
            dma((7,)),
        ],
        compiler_params=pltpu.CompilerParams(
            collective_id=0, has_side_effects=True, vmem_limit_bytes=62 * 2**20
        ),
        cost_estimate=pl.CostEstimate(
            flops=6 * TOK * D * COLS, bytes_accessed=2**24, transcendentals=2 * TOK * COLS
        ),
        name="exchange",
    )(tokens, weight, cotangent, left_stats, right_stats)


def precondition_kernel(
    gt_ref, left_ref, right_ref, tg_ref, up_ref, lnew_ref, rnew_ref,
    tg_out, update_ref, left_out, right_out,
    up, lnew, rnew, sems,
):
    def move(i, source, target):
        copy = pltpu.make_async_copy(source, target, sems.at[i])
        copy.start()
        return copy

    passed = [
        move(0, tg_ref, tg_out),
        move(1, up_ref, update_ref.at[:, pl.ds(0, BLK)]),
        move(2, lnew_ref, left_out.at[0, 0]),
        move(3, rnew_ref, right_out.at[0, 0]),
    ]
    gt = gt_ref[...]
    grad = gt.T
    gth, gh = gt.astype(BF16), grad.astype(BF16)
    rows = lax.broadcasted_iota(jnp.int32, (BLK, BLK), 0)
    cols = lax.broadcasted_iota(jnp.int32, (BLK, BLK), 1)
    eye = jnp.where(rows == cols, 1.0, 0.0).astype(F32)
    share = (1.0 - decay_rate) / BLK
    left = decay_rate * left_ref[0, 0] + share * dot(gh, gth)
    right = decay_rate * right_ref[0, 0] + share * dot(gth, gh)
    lnew[...] = left
    rnew[...] = right
    passed.append(move(4, lnew, left_out.at[0, 1]))
    passed.append(move(5, rnew, right_out.at[0, 1]))

    def each(function, *lists):
        return [function(*items) for items in zip(*lists)]

    def start(stat):
        trace = total_of(stat * eye)
        regular = stat + (ridge_share * trace / BLK) * eye
        scale = jnp.sqrt(total_of(regular * regular)) / 4.0
        return regular / scale, scale

    begun = each(start, (left, right))
    first = [b[0] for b in begun]
    scales = [b[1] for b in begun]
    firsth = each(lambda a: a.astype(BF16), first)
    square = each(dot, firsth, firsth)
    zero_sq = each(
        lambda a, q: (1.5625 * eye - 0.625 * a + 0.0625 * q).astype(BF16), first, square
    )
    crossed = each(lambda a, q: (1.25 * a - 0.25 * q).astype(BF16), first, square)
    fourth = each(lambda a: dot(a, a).astype(BF16), zero_sq)
    two = each(
        lambda a, f, x: 1.5625 * eye - 0.3125 * a - 0.25 * dot(f, x), first, fourth, crossed
    )
    twoh = each(lambda a: a.astype(BF16), two)
    two_sq = each(lambda a: dot(a, a).astype(BF16), twoh)
    two_crossed = each(lambda a, f: dot(a, f).astype(BF16), twoh, firsth)
    two_fourth = each(lambda a: dot(a, a).astype(BF16), two_sq)
    roots = each(
        lambda a, f, x, s: (
            lax.rsqrt(jnp.sqrt(s)) * (1.25 * a - 0.25 * dot(f, x))
        ).astype(BF16),
        two, two_fourth, two_crossed, scales,
    )
    left_part = dot(roots[0], gh).astype(BF16)
    raw = dot(left_part, roots[1])
    size = float(BLK * BLK)
    grad_rms = jnp.sqrt(total_of(gt * gt) / size)
    raw_rms = jnp.sqrt(total_of(raw * raw) / size + epsilon)
    up[...] = (raw * (grad_rms / raw_rms)).astype(BF16)
    passed.append(move(6, up, update_ref.at[:, pl.ds(BLK, BLK)]))
    for copy in passed:
        copy.wait()


def precondition(gt, left_stats, right_stats, tokens_grad, up, left_new, right_new):
    any_spec = pl.BlockSpec(memory_space=pl.ANY)
    stat_spec = pl.BlockSpec((1, 1, BLK, BLK), lambda i: (0, 1, 0, 0))
    return pl.pallas_call(
        precondition_kernel,
        grid=(1,),
        out_shape=(
            jax.ShapeDtypeStruct((TOK, FEAT), BF16),
            jax.ShapeDtypeStruct((BLK, COLS), BF16),
            jax.ShapeDtypeStruct(left_stats.shape, F32),
            jax.ShapeDtypeStruct(right_stats.shape, F32),
        ),
        in_specs=[pl.BlockSpec((BLK, BLK), lambda i: (0, 0)), stat_spec, stat_spec]
        + [any_spec] * 4,
        out_specs=(any_spec,) * 4,
        scratch_shapes=[
            pltpu.VMEM((BLK, BLK), BF16),
            pltpu.VMEM((BLK, BLK), F32),
            pltpu.VMEM((BLK, BLK), F32),
            pltpu.SemaphoreType.DMA((7,)),
        ],
        compiler_params=pltpu.CompilerParams(vmem_limit_bytes=48 * 2**20),
        name="precondition",
    )(gt, left_stats, right_stats, tokens_grad, up, left_new, right_new)


def shards(tokens, weight, cotangent, left_stats, right_stats):
    tokens_grad, gt, up, left_half, right_half = exchange(
        tokens, weight, cotangent, left_stats, right_stats
    )
    return precondition(gt, left_stats, right_stats, tokens_grad, up, left_half, right_half)


def solution(mesh):
    two = P("dp", ("tensor", "pre"))
    four = P("dp", ("tensor", "pre"), None, None)
    return jax.shard_map(
        shards,
        mesh=mesh,
        in_specs=(two, two, two, four, four),
        out_specs=(two, two, four, four),
        check_vma=False,
    )
```

```python
import jax
import jax.numpy as jnp
from jax import lax
from jax.experimental import pallas as pl
from jax.experimental.pallas import tpu as pltpu
from jax.sharding import PartitionSpec as P

MESH = pl.DeviceIdType.MESH
F32 = jnp.float32
BF16 = jnp.bfloat16

TOK = 1024
D = 4096
BLK = 512
COLS = 1024
FEAT = 256

decay_rate = 0.5
ridge_share = 0.05
epsilon = 1e-06
grad_scale = float(8192) ** (-0.5)

XA = (0, 176)
ZA = (176, 80)
ZB = (256, 80)
XB = (336, 176)
ZZ = (176, 160)
HA = (0, 256)
HB = (256, 256)
N_SEND = 86
N_RECV = 126


def dot(a, b):
    return jnp.dot(a, b, preferred_element_type=F32)


def gelu_slope(values):
    return (
        0.5 * (1.0 + lax.erf(values * 0.7071067811865476))
        + values * jnp.exp(-0.5 * values * values) * 0.3989422804014327
    )


def add_rows(dst, sources, rows, chunk=16):
    def body(i, carry):
        at = pl.ds(pl.multiple_of(i * chunk, chunk), chunk)
        total = sources[0][at, :].astype(F32)
        for source in sources[1:]:
            total = total + source[at, :].astype(F32)
        dst[at, :] = total.astype(dst.dtype)
        return carry

    lax.fori_loop(0, rows // chunk, body, 0)


def total_of(values):
    return jnp.sum(jnp.sum(values, axis=1, keepdims=True), axis=0, keepdims=True)


def exchange_kernel(
    tok_ref, w_ref, cot_ref, left_ref, right_ref, tg_ref, gt_ref, up_ref, lnew_ref, rnew_ref,
    wf, tok, hg, hgt, hid, part, dout,
    s1, s1z, s2, s2z, rz, rx, sib, t1, t2, tx, gt0, stat, work,
    ss, rs, ls,
):
    dp = lax.axis_index("dp")
    tn = lax.axis_index("tensor")
    c = lax.axis_index("pre")
    z, l = lax.div(dp, 2), lax.rem(dp, 2)
    xh, y = lax.div(tn, 4), lax.rem(tn, 4)
    m = 1 - l
    up, um, u2 = lax.rem(z + 1, 4), lax.rem(z + 3, 4), lax.rem(z + 2, 4)
    yp, ym, y2 = lax.rem(y + 1, 4), lax.rem(y + 3, 4), lax.rem(y + 2, 4)
    oh, oc = 1 - xh, 1 - c
    dev_zp, dev_zm = (up * 2 + l, tn, c), (um * 2 + l, tn, c)
    dev_x = (z * 2 + m, tn, c)
    dev_yp, dev_ym = (dp, xh * 4 + yp, c), (dp, xh * 4 + ym, c)
    dev_h = (dp, oh * 4 + y, c)
    dev_c = (dp, tn, oc)

    barrier = pltpu.get_barrier_semaphore()
    for dev in (dev_zp, dev_zm, dev_x, dev_yp, dev_ym, dev_h, dev_c):
        pl.semaphore_signal(barrier, inc=1, device_id=dev, device_id_type=MESH)
    pl.semaphore_wait(barrier, 7)

    copies, pending = [], []
    unused = list(range(N_SEND))

    def send(src, dst, dev):
        k = unused.pop(0)
        copy = pltpu.make_async_remote_copy(
            src_ref=src, dst_ref=dst, send_sem=ss.at[k], recv_sem=rs.at[len(copies)],
            device_id=dev, device_id_type=MESH,
        )
        copy.start()
        copies.append(copy)
        pending.append((copy, k))
        return copy

    def release():
        for copy, k in pending:
            copy.wait_send()
            unused.append(k)
        pending.clear()

    def got(*several):
        for copy in several:
            copy.wait_recv()

    def rows_of(zi, li, rows):
        return pl.ds(pl.multiple_of((zi * 2 + li) * BLK + rows[0], 16), rows[1])

    def wpart(zi, li, rows, h):
        return wf.at[rows_of(zi, li, rows), pl.ds(h * BLK, BLK)]

    def wsend(zi, li, rows, h, dev):
        ref = wpart(zi, li, rows, h)
        return send(ref, ref, dev)

    wstate = [dict(), dict()]

    def w_own(h, first):
        q = wstate[h]

        def own(rows, dev):
            return send(
                w_ref.at[pl.ds(rows[0], rows[1]), pl.ds(h * BLK, BLK)],
                wpart(z, l, rows, h), dev,
            )

        if first:
            q["pa"], q["mb"] = own(HA, dev_zp), own(HB, dev_zm)
            q["xa"], q["xb"] = own(XA, dev_x), own(XB, dev_x)
        else:
            q["pb"], q["ma"] = own(HB, dev_zp), own(HA, dev_zm)
            q["xz"] = own(ZZ, dev_x)

    def w_partner(h):
        q = wstate[h]
        got(q["xa"])
        q["ppa"] = wsend(z, m, XA, h, dev_zp)
        got(q["xb"])
        q["pmb"] = wsend(z, m, XB, h, dev_zm)
        q["ppb"] = wsend(z, m, XB, h, dev_zp)
        q["pma"] = wsend(z, m, XA, h, dev_zm)

    def w_forward_own(h):
        q = wstate[h]
        got(q["pa"])
        q["fa"] = wsend(um, l, HA, h, dev_zp)
        got(q["mb"])
        q["fb"] = wsend(up, l, HB, h, dev_zm)

    def w_cross(h):
        q = wstate[h]
        got(q["pb"])
        q["xzm"] = wsend(um, l, ZZ, h, dev_x)
        got(q["ma"])
        q["xzp"] = wsend(up, l, ZZ, h, dev_x)

    def w_forward_partner(h):
        q = wstate[h]
        got(q["ppa"])
        q["fpa"] = wsend(um, m, XA, h, dev_zp)
        got(q["pmb"])
        q["fpb"] = wsend(up, m, XB, h, dev_zm)

    def w_last(h):
        q = wstate[h]
        got(q["fa"])
        q["x2a"] = wsend(u2, l, ZA, h, dev_x)
        got(q["fb"])
        q["x2b"] = wsend(u2, l, ZB, h, dev_x)

    def w_done(h):
        q = wstate[h]
        got(*(q[k] for k in ("xz", "ppb", "pma", "xzm", "xzp", "fpa", "fpb", "x2a", "x2b")))

    TA, TB = pl.ds(0, TOK // 2), pl.ds(TOK // 2, TOK // 2)
    ALL = pl.ds(0, TOK)

    def tcols(hi, yi, ci):
        return pl.ds(pl.multiple_of(((hi * 4 + yi) * 2 + ci) * FEAT, FEAT), FEAT)

    def tsend(hi, yi, rows, dev):
        ref = tok.at[rows, tcols(hi, yi, c)]
        return send(ref, ref, dev)

    tq = {}

    def t_own():
        def own(rows, dev):
            return send(tok_ref.at[rows, :], tok.at[rows, tcols(xh, y, c)], dev)

        tq["h"] = own(ALL, dev_h)
        tq["pa"], tq["mb"] = own(TA, dev_yp), own(TB, dev_ym)
        tq["pb"], tq["ma"] = own(TB, dev_yp), own(TA, dev_ym)
        tq["c0"] = own(ALL, dev_c)

    def t_partner():
        got(tq["h"])
        tq["hpa"], tq["hmb"] = tsend(oh, y, TA, dev_yp), tsend(oh, y, TB, dev_ym)
        tq["hpb"], tq["hma"] = tsend(oh, y, TB, dev_yp), tsend(oh, y, TA, dev_ym)
        tq["c1"] = tsend(oh, y, ALL, dev_c)

    def t_forward_own():
        got(tq["pa"])
        tq["fa"] = tsend(xh, ym, TA, dev_yp)
        got(tq["mb"])
        tq["fb"] = tsend(xh, yp, TB, dev_ym)

    def t_share_own():
        got(tq["pb"])
        tq["c2"] = tsend(xh, ym, ALL, dev_c)
        got(tq["ma"])
        tq["c3"] = tsend(xh, yp, ALL, dev_c)

    def t_forward_partner():
        got(tq["hpa"])
        tq["hfa"] = tsend(oh, ym, TA, dev_yp)
        got(tq["hmb"])
        tq["hfb"] = tsend(oh, yp, TB, dev_ym)
        got(tq["hpb"])
        tq["c4"] = tsend(oh, ym, ALL, dev_c)
        got(tq["hma"])
        tq["c5"] = tsend(oh, yp, ALL, dev_c)

    def t_last_own():
        got(tq["fa"], tq["fb"])
        tq["c6"] = tsend(xh, y2, ALL, dev_c)

    def t_last():
        got(tq["hfa"], tq["hfb"])
        tq["c7"] = tsend(oh, y2, ALL, dev_c)

    def t_done():
        got(*(tq["c%d" % i] for i in range(8)))

    dq = {}

    def hidden(h, r):
        cols = pl.ds(h * BLK, BLK)

        def tile(i, carry):
            at = pl.ds(pl.multiple_of(i * 256, 256), 256)
            hid[...] = dot(tok[at, :], wf[:, cols])

            def slope(j, inner):
                small = pl.ds(pl.multiple_of(j * 16, 16), 16)
                big = pl.ds(pl.multiple_of(i * 256 + j * 16, 16), 16)
                cot = hg[big, cols].astype(F32)
                hg[big, cols] = (cot * gelu_slope(hid[small, :])).astype(BF16)
                return inner

            lax.fori_loop(0, 16, slope, 0, unroll=4)
            return carry

        lax.fori_loop(2 * r, 2 * r + 2, tile, 0)

    def gradient(h):
        cols = pl.ds(h * BLK, BLK)
        for i in range(4):
            at = pl.ds(i * 256, 256)
            hgt[:, at] = hg[at, cols].T

        def block(d, carry):
            at = pl.ds(pl.multiple_of(d * BLK, BLK), BLK)
            part[h, d] = (dot(hgt[...], tok[:, at]) * grad_scale).astype(BF16)
            return carry

        lax.fori_loop(0, 8, block, 0, unroll=8)

    def wide_dot(rows, g):
        at = pl.ds(pl.multiple_of(g * FEAT, FEAT), FEAT)
        return lax.dot_general(
            hg[rows, :], wf[at, :], (((1,), (1,)), ((), ())), preferred_element_type=F32
        )

    def input_other(r):
        rows = pl.ds(r * (TOK // 2), TOK // 2)

        def block(t, carry):
            dout[t, rows, :] = wide_dot(rows, t * 2 + oc).astype(BF16)
            return carry

        lax.fori_loop(0, 8, block, 0, unroll=8)
        dq["c", r] = send(dout.at[:, rows, :], sib.at[:, rows, :], dev_c)

    def input_own(r):
        got(dq["c", r])
        rows = pl.ds(r * (TOK // 2), TOK // 2)

        def block(t, carry):
            mine = wide_dot(rows, t * 2 + c) + sib[t, rows, :].astype(F32)
            sib[t, rows, :] = mine.astype(BF16)
            return carry

        lax.fori_loop(0, 8, block, 0, unroll=8)

    def ppart(h, zi, li, rows):
        return part.at[h, zi * 2 + li, pl.ds(rows[0], rows[1]), :]

    gstate = [dict(), dict()]
    OTHER, OWN = 0, 1
    DN, UP = 0, 1

    def g_start(h):
        q = gstate[h]
        for zi, name in ((u2, "rz2"), (up, "rzp"), (um, "rzm"), (z, "rz0")):
            q[name] = send(ppart(h, zi, m, ZZ), rz.at[h, zi], dev_x)
        for side, li in ((OTHER, m), (OWN, l)):
            q["1p", side] = send(ppart(h, u2, li, XA), s1.at[h, UP, side], dev_zp)
            q["1m", side] = send(ppart(h, u2, li, XB), s1.at[h, DN, side], dev_zm)
        for side, li in ((OTHER, m), (OWN, l)):
            q["2pb", side] = send(ppart(h, up, li, XB), s2.at[h, UP, side, 1], dev_zp)
            q["2ma", side] = send(ppart(h, um, li, XA), s2.at[h, DN, side, 0], dev_zm)

    def g_second(h):
        q = gstate[h]
        for side, li in ((OTHER, m), (OWN, l)):
            got(q["1p", side])
            mine = ppart(h, up, li, XA)
            add_rows(mine, (mine, s1.at[h, UP, side]), XA[1])
            q["2pa", side] = send(mine, s2.at[h, UP, side, 0], dev_zp)
            got(q["1m", side])
            mine = ppart(h, um, li, XB)
            add_rows(mine, (mine, s1.at[h, DN, side]), XB[1])
            q["2mb", side] = send(mine, s2.at[h, DN, side, 1], dev_zm)

    def g_middle(h):
        q = gstate[h]
        for zi, name in ((u2, "rz2"), (up, "rzp"), (um, "rzm"), (z, "rz0")):
            got(q[name])
            mine = ppart(h, zi, l, ZZ)
            add_rows(mine, (mine, rz.at[h, zi]), ZZ[1])
        q["z1p"] = send(ppart(h, u2, l, ZA), s1z.at[h, UP], dev_zp)
        q["z1m"] = send(ppart(h, u2, l, ZB), s1z.at[h, DN], dev_zm)
        q["z2pb"] = send(ppart(h, up, l, ZB), s2z.at[h, UP, 1], dev_zp)
        q["z2ma"] = send(ppart(h, um, l, ZA), s2z.at[h, DN, 0], dev_zm)

    def g_middle_second(h):
        q = gstate[h]
        got(q["z1p"])
        mine = ppart(h, up, l, ZA)
        add_rows(mine, (mine, s1z.at[h, UP]), ZA[1])
        q["z2pa"] = send(mine, s2z.at[h, UP, 0], dev_zp)
        got(q["z1m"])
        mine = ppart(h, um, l, ZB)
        add_rows(mine, (mine, s1z.at[h, DN]), ZB[1])
        q["z2mb"] = send(mine, s2z.at[h, DN, 1], dev_zm)

    def g_cross(h):
        q = gstate[h]
        for k, rows, name in ((0, XA, "a"), (1, XB, "b")):
            got(q["2p" + name, OTHER], q["2m" + name, OTHER])
            mine = ppart(h, z, m, rows)
            add_rows(mine, (mine, s2.at[h, UP, OTHER, k], s2.at[h, DN, OTHER, k]), rows[1])
            q["x" + name] = send(mine, rx.at[h, k], dev_x)

    def g_final(h):
        q = gstate[h]
        out = gt0 if h == 0 else gt_ref
        for k, rows, name in ((0, ZA, "a"), (1, ZB, "b")):
            got(q["z2p" + name], q["z2m" + name])
            add_rows(
                out.at[pl.ds(rows[0], rows[1]), :],
                (ppart(h, z, l, rows), s2z.at[h, UP, k], s2z.at[h, DN, k]),
                rows[1],
            )
        for k, rows, name in ((0, XA, "a"), (1, XB, "b")):
            got(q["2p" + name, OWN], q["2m" + name, OWN], q["x" + name])
            add_rows(
                out.at[pl.ds(rows[0], rows[1]), :],
                (ppart(h, z, l, rows), s2.at[h, UP, OWN, k], s2.at[h, DN, OWN, k], rx.at[h, k]),
                rows[1],
            )

    def dpart(hi, yi, ci, rows):
        return sib.at[hi * 4 + yi, rows, :]

    sides = ((OTHER, oh), (OWN, xh))

    def d_first(r):
        for side, hi in sides:
            if r == 0:
                dq["1p", side] = send(dpart(hi, y2, c, TA), t1.at[UP, side], dev_yp)
                dq["2ma", side] = send(dpart(hi, ym, c, TA), t2.at[DN, side, 0], dev_ym)
            else:
                dq["1m", side] = send(dpart(hi, y2, c, TB), t1.at[DN, side], dev_ym)
                dq["2pb", side] = send(dpart(hi, yp, c, TB), t2.at[UP, side, 1], dev_yp)

    def d_second():
        for side, hi in sides:
            got(dq["1p", side])
            mine = dpart(hi, yp, c, TA)
            add_rows(mine, (mine, t1.at[UP, side]), TOK // 2)
            dq["2pa", side] = send(mine, t2.at[UP, side, 0], dev_yp)
            got(dq["1m", side])
            mine = dpart(hi, ym, c, TB)
            add_rows(mine, (mine, t1.at[DN, side]), TOK // 2)
            dq["2mb", side] = send(mine, t2.at[DN, side, 1], dev_ym)

    def d_cross():
        for k, rows, name in ((0, TA, "a"), (1, TB, "b")):
            got(dq["2p" + name, OTHER], dq["2m" + name, OTHER])
            mine = dpart(oh, y, c, rows)
            add_rows(mine, (mine, t2.at[UP, OTHER, k], t2.at[DN, OTHER, k]), TOK // 2)
            dq["x" + name] = send(mine, tx.at[k], dev_h)

    def d_final():
        for k, rows, name in ((0, TA, "a"), (1, TB, "b")):
            got(dq["2p" + name, OWN], dq["2m" + name, OWN], dq["x" + name])
            add_rows(
                tg_ref.at[rows, :],
                (dpart(xh, y, c, rows), t2.at[UP, OWN, k], t2.at[DN, OWN, k], tx.at[k]),
                TOK // 2,
            )

    def newton(h):
        for copy in held:
            copy.wait()

        slots = iter(
            [wf.at[pl.ds(i * BLK, BLK), pl.ds(j * BLK, BLK)] for i in range(8) for j in range(2)]
            + [tok.at[pl.ds(0, BLK), pl.ds(j * BLK, BLK)] for j in range(8)]
        )
        gh, gth, lp = next(slots), next(slots), next(slots)
        mh, zs, cr, fo, tw, tq2, tc, tf, root = [(next(slots), next(slots)) for _ in range(9)]
        pieces = [pl.ds(i * 256, 256) for i in range(2)]
        ids = lax.broadcasted_iota(jnp.int32, (256, BLK), 0)
        across = lax.broadcasted_iota(jnp.int32, (256, BLK), 1)
        eyes = [jnp.where(ids + i * 256 == across, 1.0, 0.0).astype(F32) for i in range(2)]
        share = (1.0 - decay_rate) / BLK

        gth[...] = gt0[...].astype(BF16)
        gh[...] = gt0[...].T.astype(BF16)
        trace, norm = [0.0, 0.0], [0.0, 0.0]
        for i, rows in enumerate(pieces):
            for side, (a, b) in enumerate(((gh, gth), (gth, gh))):
                new = decay_rate * stat[side, rows, :] + share * dot(a[rows, :], b[...])
                stat[side, rows, :] = new
                trace[side] += total_of(new * eyes[i])
                norm[side] += total_of(new * new)
        for side, out in enumerate((lnew_ref, rnew_ref)):
            back = pltpu.make_async_copy(stat.at[side], out, ls.at[5 + side])
            back.start()
            backs.append(back)
        scale = [None, None]
        for side in range(2):
            ridge = ridge_share * trace[side] / BLK
            full = norm[side] + 2.0 * ridge * trace[side] + BLK * ridge * ridge
            scale[side] = jnp.sqrt(full) / 4.0
            for i, rows in enumerate(pieces):
                first = (stat[side, rows, :] + ridge * eyes[i]) / scale[side]
                work[side, rows, :] = first
                mh[side][rows, :] = first.astype(BF16)
        for i, rows in enumerate(pieces):
            for side in range(2):
                first = work[side, rows, :]
                square = dot(mh[side][rows, :], mh[side][...])
                zs[side][rows, :] = (1.5625 * eyes[i] - 0.625 * first + 0.0625 * square).astype(BF16)
                cr[side][rows, :] = (1.25 * first - 0.25 * square).astype(BF16)
        for rows in pieces:
            for side in range(2):
                fo[side][rows, :] = dot(zs[side][rows, :], zs[side][...]).astype(BF16)
        for i, rows in enumerate(pieces):
            for side in range(2):
                two = (
                    1.5625 * eyes[i]
                    - 0.3125 * work[side, rows, :]
                    - 0.25 * dot(fo[side][rows, :], cr[side][...])
                )
                work[side, rows, :] = two
                tw[side][rows, :] = two.astype(BF16)
        for rows in pieces:
            for side in range(2):
                tq2[side][rows, :] = dot(tw[side][rows, :], tw[side][...]).astype(BF16)
                tc[side][rows, :] = dot(tw[side][rows, :], mh[side][...]).astype(BF16)
        for rows in pieces:
            for side in range(2):
                tf[side][rows, :] = dot(tq2[side][rows, :], tq2[side][...]).astype(BF16)
        for rows in pieces:
            for side in range(2):
                three = 1.25 * work[side, rows, :] - 0.25 * dot(tf[side][rows, :], tc[side][...])
                root[side][rows, :] = (lax.rsqrt(jnp.sqrt(scale[side])) * three).astype(BF16)
        for rows in pieces:
            lp[rows, :] = dot(root[0][rows, :], gh[...]).astype(BF16)
        raw_sum, grad_sum = 0.0, 0.0
        for rows in pieces:
            raw = dot(lp[rows, :], root[1][...])
            work[0, rows, :] = raw
            raw_sum += total_of(raw * raw)
            grad_sum += total_of(gt0[rows, :] * gt0[rows, :])
        size = float(BLK * BLK)
        ratio = jnp.sqrt(grad_sum / size) / jnp.sqrt(raw_sum / size + epsilon)
        for rows in pieces:
            up_ref[rows, :] = (work[0, rows, :] * ratio).astype(BF16)

    local = [
        pltpu.make_async_copy(w_ref, wf.at[rows_of(z, l, (0, BLK)), :], ls.at[0]),
        pltpu.make_async_copy(tok_ref, tok.at[:, tcols(xh, y, c)], ls.at[1]),
        pltpu.make_async_copy(cot_ref, hg, ls.at[2]),
    ]
    held = [
        pltpu.make_async_copy(left_ref.at[0, 0], stat.at[0], ls.at[3]),
        pltpu.make_async_copy(right_ref.at[0, 0], stat.at[1], ls.at[4]),
    ]
    backs = []
    w_own(1, False)
    t_own()
    w_own(0, True)
    t_forward_own()
    for copy in local + held:
        copy.start()
    w_own(1, True)
    w_forward_own(0)
    w_own(0, False)
    t_last_own()
    w_partner(0)
    w_last(0)
    w_forward_own(1)
    t_partner()
    w_cross(0)
    w_forward_partner(0)
    w_partner(1)
    t_forward_partner()
    t_last()
    t_share_own()
    w_last(1)
    t_done()
    w_done(0)
    w_cross(1)
    for copy in local:
        copy.wait()
    hidden(0, 0)
    w_forward_partner(1)
    hidden(0, 1)
    gradient(0)
    g_start(0)
    w_done(1)
    hidden(1, 0)
    input_other(0)
    hidden(1, 1)
    input_other(1)
    input_own(0)
    d_first(0)
    g_second(0)
    release()
    gradient(1)
    g_middle(0)
    g_start(1)
    input_own(1)
    d_first(1)
    g_cross(0)
    d_second()
    g_middle_second(0)
    g_second(1)
    d_cross()
    g_final(0)
    g_middle(1)
    g_cross(1)
    newton(0)
    g_middle_second(1)
    d_final()
    g_final(1)
    for copy in backs:
        copy.wait()
    release()


def exchange(tokens, weight, cotangent, left_stats, right_stats):
    any_spec = pl.BlockSpec(memory_space=pl.ANY)
    vmem_spec = pl.BlockSpec(memory_space=pltpu.VMEM)
    dma = pltpu.SemaphoreType.DMA
    square = jax.ShapeDtypeStruct((BLK, BLK), F32)
    return pl.pallas_call(
        exchange_kernel,
        out_shape=(
            jax.ShapeDtypeStruct((TOK, FEAT), BF16),
            square,
            jax.ShapeDtypeStruct((BLK, BLK), BF16),
            square,
            square,
        ),
        in_specs=[any_spec] * 5,
        out_specs=(vmem_spec, vmem_spec, vmem_spec, any_spec, any_spec),
        scratch_shapes=[
            pltpu.VMEM((D, COLS), BF16),
            pltpu.VMEM((TOK, D), BF16),
            pltpu.VMEM((TOK, COLS), BF16),
            pltpu.VMEM((BLK, TOK), BF16),
            pltpu.VMEM((256, BLK), F32),
            pltpu.VMEM((2, 8, BLK, BLK), BF16),
            pltpu.VMEM((8, TOK, FEAT), BF16),
            pltpu.VMEM((2, 2, 2, XA[1], BLK), BF16),
            pltpu.VMEM((2, 2, ZA[1], BLK), BF16),
            pltpu.VMEM((2, 2, 2, 2, XA[1], BLK), BF16),
            pltpu.VMEM((2, 2, 2, ZA[1], BLK), BF16),
            pltpu.VMEM((2, 4, ZZ[1], BLK), BF16),
            pltpu.VMEM((2, 2, XA[1], BLK), BF16),
            pltpu.VMEM((8, TOK, FEAT), BF16),
            pltpu.VMEM((2, 2, TOK // 2, FEAT), BF16),
            pltpu.VMEM((2, 2, 2, TOK // 2, FEAT), BF16),
            pltpu.VMEM((2, TOK // 2, FEAT), BF16),
            pltpu.VMEM((BLK, BLK), F32),
            pltpu.VMEM((2, BLK, BLK), F32),
            pltpu.VMEM((2, BLK, BLK), F32),
            dma((N_SEND,)),
            dma((N_RECV,)),
            dma((7,)),
        ],
        compiler_params=pltpu.CompilerParams(
            collective_id=0, has_side_effects=True, vmem_limit_bytes=62 * 2**20
        ),
        cost_estimate=pl.CostEstimate(
            flops=6 * TOK * D * COLS, bytes_accessed=2**24, transcendentals=2 * TOK * COLS
        ),
        name="exchange",
    )(tokens, weight, cotangent, left_stats, right_stats)


def precondition_kernel(
    gt_ref, left_ref, right_ref, tg_ref, up_ref, lnew_ref, rnew_ref,
    tg_out, update_ref, left_out, right_out,
    up, lnew, rnew, tg_held, up_held, l_held, r_held, sems,
):
    def move(i, source, target):
        copy = pltpu.make_async_copy(source, target, sems.at[i])
        copy.start()
        return copy

    holds = (
        (tg_ref, tg_held, tg_out),
        (up_ref, up_held, update_ref.at[:, pl.ds(0, BLK)]),
        (lnew_ref, l_held, left_out.at[0, 0]),
        (rnew_ref, r_held, right_out.at[0, 0]),
    )
    arriving = [move(i, source, held) for i, (source, held, _) in enumerate(holds)]
    passed = []
    gt = gt_ref[...]
    grad = gt.T
    gth, gh = gt.astype(BF16), grad.astype(BF16)
    rows = lax.broadcasted_iota(jnp.int32, (BLK, BLK), 0)
    cols = lax.broadcasted_iota(jnp.int32, (BLK, BLK), 1)
    eye = jnp.where(rows == cols, 1.0, 0.0).astype(F32)
    share = (1.0 - decay_rate) / BLK
    left = decay_rate * left_ref[0, 0] + share * dot(gh, gth)
    right = decay_rate * right_ref[0, 0] + share * dot(gth, gh)
    lnew[...] = left
    rnew[...] = right
    for i, (copy, (_, held, target)) in enumerate(zip(arriving, holds)):
        copy.wait()
        passed.append(move(7 + i, held, target))
    passed.append(move(4, lnew, left_out.at[0, 1]))
    passed.append(move(5, rnew, right_out.at[0, 1]))

    def each(function, *lists):
        return [function(*items) for items in zip(*lists)]

    def start(stat):
        trace = total_of(stat * eye)
        regular = stat + (ridge_share * trace / BLK) * eye
        scale = jnp.sqrt(total_of(regular * regular)) / 4.0
        return regular / scale, scale

    begun = each(start, (left, right))
    first = [b[0] for b in begun]
    scales = [b[1] for b in begun]
    firsth = each(lambda a: a.astype(BF16), first)
    square = each(dot, firsth, firsth)
    zero_sq = each(
        lambda a, q: (1.5625 * eye - 0.625 * a + 0.0625 * q).astype(BF16), first, square
    )
    crossed = each(lambda a, q: (1.25 * a - 0.25 * q).astype(BF16), first, square)
    fourth = each(lambda a: dot(a, a).astype(BF16), zero_sq)
    two = each(
        lambda a, f, x: 1.5625 * eye - 0.3125 * a - 0.25 * dot(f, x), first, fourth, crossed
    )
    twoh = each(lambda a: a.astype(BF16), two)
    two_sq = each(lambda a: dot(a, a).astype(BF16), twoh)
    two_crossed = each(lambda a, f: dot(a, f).astype(BF16), twoh, firsth)
    two_fourth = each(lambda a: dot(a, a).astype(BF16), two_sq)
    roots = each(
        lambda a, f, x, s: (
            lax.rsqrt(jnp.sqrt(s)) * (1.25 * a - 0.25 * dot(f, x))
        ).astype(BF16),
        two, two_fourth, two_crossed, scales,
    )
    left_part = dot(roots[0], gh).astype(BF16)
    raw = dot(left_part, roots[1])
    size = float(BLK * BLK)
    grad_rms = jnp.sqrt(total_of(gt * gt) / size)
    raw_rms = jnp.sqrt(total_of(raw * raw) / size + epsilon)
    up[...] = (raw * (grad_rms / raw_rms)).astype(BF16)
    passed.append(move(6, up, update_ref.at[:, pl.ds(BLK, BLK)]))
    for copy in passed:
        copy.wait()


def precondition(gt, left_stats, right_stats, tokens_grad, up, left_new, right_new):
    any_spec = pl.BlockSpec(memory_space=pl.ANY)
    stat_spec = pl.BlockSpec((1, 1, BLK, BLK), lambda i: (0, 1, 0, 0))
    return pl.pallas_call(
        precondition_kernel,
        grid=(1,),
        out_shape=(
            jax.ShapeDtypeStruct((TOK, FEAT), BF16),
            jax.ShapeDtypeStruct((BLK, COLS), BF16),
            jax.ShapeDtypeStruct(left_stats.shape, F32),
            jax.ShapeDtypeStruct(right_stats.shape, F32),
        ),
        in_specs=[pl.BlockSpec((BLK, BLK), lambda i: (0, 0)), stat_spec, stat_spec]
        + [any_spec] * 4,
        out_specs=(any_spec,) * 4,
        scratch_shapes=[
            pltpu.VMEM((BLK, BLK), BF16),
            pltpu.VMEM((BLK, BLK), F32),
            pltpu.VMEM((BLK, BLK), F32),
            pltpu.VMEM((TOK, FEAT), BF16),
            pltpu.VMEM((BLK, BLK), BF16),
            pltpu.VMEM((BLK, BLK), F32),
            pltpu.VMEM((BLK, BLK), F32),
            pltpu.SemaphoreType.DMA((11,)),
        ],
        compiler_params=pltpu.CompilerParams(vmem_limit_bytes=62 * 2**20),
        name="precondition",
    )(gt, left_stats, right_stats, tokens_grad, up, left_new, right_new)


def shards(tokens, weight, cotangent, left_stats, right_stats):
    tokens_grad, gt, up, left_half, right_half = exchange(
        tokens, weight, cotangent, left_stats, right_stats
    )
    return precondition(gt, left_stats, right_stats, tokens_grad, up, left_half, right_half)


def solution(mesh):
    two = P("dp", ("tensor", "pre"))
    four = P("dp", ("tensor", "pre"), None, None)
    return jax.shard_map(
        shards,
        mesh=mesh,
        in_specs=(two, two, two, four, four),
        out_specs=(two, two, four, four),
        check_vma=False,
    )
```

```python
import jax
import jax.numpy as jnp
from jax import lax
from jax.experimental import pallas as pl
from jax.experimental.pallas import tpu as pltpu
from jax.sharding import PartitionSpec as P

MESH = pl.DeviceIdType.MESH
F32 = jnp.float32
BF16 = jnp.bfloat16

TOK = 1024
D = 4096
BLK = 512
COLS = 1024
FEAT = 256

decay_rate = 0.5
ridge_share = 0.05
epsilon = 1e-06
grad_scale = float(8192) ** (-0.5)

XA = (0, 176)
ZA = (176, 80)
ZB = (256, 80)
XB = (336, 176)
ZZ = (176, 160)
HA = (0, 256)
HB = (256, 256)
N_SEND = 86
N_RECV = 126


def dot(a, b):
    return jnp.dot(a, b, preferred_element_type=F32)


def gelu_slope(values):
    return (
        0.5 * (1.0 + lax.erf(values * 0.7071067811865476))
        + values * jnp.exp(-0.5 * values * values) * 0.3989422804014327
    )


def add_rows(dst, sources, rows, chunk=16):
    def body(i, carry):
        at = pl.ds(pl.multiple_of(i * chunk, chunk), chunk)
        total = sources[0][at, :].astype(F32)
        for source in sources[1:]:
            total = total + source[at, :].astype(F32)
        dst[at, :] = total.astype(dst.dtype)
        return carry

    lax.fori_loop(0, rows // chunk, body, 0)


def total_of(values):
    return jnp.sum(jnp.sum(values, axis=1, keepdims=True), axis=0, keepdims=True)


def exchange_kernel(
    tok_ref, w_ref, cot_ref, left_ref, right_ref, tg_ref, gt_ref, up_ref, lnew_ref, rnew_ref,
    wf, tok, hg, hgt, hid, part, dout,
    s1, s1z, s2, s2z, rz, rx, sib, t1, t2, tx, gt0, stat, work,
    ss, rs, ls,
):
    dp = lax.axis_index("dp")
    tn = lax.axis_index("tensor")
    c = lax.axis_index("pre")
    z, l = lax.div(dp, 2), lax.rem(dp, 2)
    xh, y = lax.div(tn, 4), lax.rem(tn, 4)
    m = 1 - l
    up, um, u2 = lax.rem(z + 1, 4), lax.rem(z + 3, 4), lax.rem(z + 2, 4)
    yp, ym, y2 = lax.rem(y + 1, 4), lax.rem(y + 3, 4), lax.rem(y + 2, 4)
    oh, oc = 1 - xh, 1 - c
    dev_zp, dev_zm = (up * 2 + l, tn, c), (um * 2 + l, tn, c)
    dev_x = (z * 2 + m, tn, c)
    dev_yp, dev_ym = (dp, xh * 4 + yp, c), (dp, xh * 4 + ym, c)
    dev_h = (dp, oh * 4 + y, c)
    dev_c = (dp, tn, oc)

    barrier = pltpu.get_barrier_semaphore()
    for dev in (dev_zp, dev_zm, dev_x, dev_yp, dev_ym, dev_h, dev_c):
        pl.semaphore_signal(barrier, inc=1, device_id=dev, device_id_type=MESH)
    pl.semaphore_wait(barrier, 7)

    copies, pending = [], []
    unused = list(range(N_SEND))

    def send(src, dst, dev):
        k = unused.pop(0)
        copy = pltpu.make_async_remote_copy(
            src_ref=src, dst_ref=dst, send_sem=ss.at[k], recv_sem=rs.at[len(copies)],
            device_id=dev, device_id_type=MESH,
        )
        copy.start()
        copies.append(copy)
        pending.append((copy, k))
        return copy

    def release():
        for copy, k in pending:
            copy.wait_send()
            unused.append(k)
        pending.clear()

    def got(*several):
        for copy in several:
            copy.wait_recv()

    def rows_of(zi, li, rows):
        return pl.ds(pl.multiple_of((zi * 2 + li) * BLK + rows[0], 16), rows[1])

    def wpart(zi, li, rows, h):
        return wf.at[rows_of(zi, li, rows), pl.ds(h * BLK, BLK)]

    def wsend(zi, li, rows, h, dev):
        ref = wpart(zi, li, rows, h)
        return send(ref, ref, dev)

    wstate = [dict(), dict()]

    def w_own(h, first):
        q = wstate[h]

        def own(rows, dev):
            return send(
                w_ref.at[pl.ds(rows[0], rows[1]), pl.ds(h * BLK, BLK)],
                wpart(z, l, rows, h), dev,
            )

        if first:
            q["pa"], q["mb"] = own(HA, dev_zp), own(HB, dev_zm)
            q["xa"], q["xb"] = own(XA, dev_x), own(XB, dev_x)
        else:
            q["pb"], q["ma"] = own(HB, dev_zp), own(HA, dev_zm)
            q["xz"] = own(ZZ, dev_x)

    def w_partner(h):
        q = wstate[h]
        got(q["xa"])
        q["ppa"] = wsend(z, m, XA, h, dev_zp)
        got(q["xb"])
        q["pmb"] = wsend(z, m, XB, h, dev_zm)
        q["ppb"] = wsend(z, m, XB, h, dev_zp)
        q["pma"] = wsend(z, m, XA, h, dev_zm)

    def w_forward_own(h):
        q = wstate[h]
        got(q["pa"])
        q["fa"] = wsend(um, l, HA, h, dev_zp)
        got(q["mb"])
        q["fb"] = wsend(up, l, HB, h, dev_zm)

    def w_cross(h):
        q = wstate[h]
        got(q["pb"])
        q["xzm"] = wsend(um, l, ZZ, h, dev_x)
        got(q["ma"])
        q["xzp"] = wsend(up, l, ZZ, h, dev_x)

    def w_forward_partner(h):
        q = wstate[h]
        got(q["ppa"])
        q["fpa"] = wsend(um, m, XA, h, dev_zp)
        got(q["pmb"])
        q["fpb"] = wsend(up, m, XB, h, dev_zm)

    def w_last(h):
        q = wstate[h]
        got(q["fa"])
        q["x2a"] = wsend(u2, l, ZA, h, dev_x)
        got(q["fb"])
        q["x2b"] = wsend(u2, l, ZB, h, dev_x)

    def w_done(h):
        q = wstate[h]
        got(*(q[k] for k in ("xz", "ppb", "pma", "xzm", "xzp", "fpa", "fpb", "x2a", "x2b")))

    TA, TB = pl.ds(0, TOK // 2), pl.ds(TOK // 2, TOK // 2)
    ALL = pl.ds(0, TOK)

    def tcols(hi, yi, ci):
        return pl.ds(pl.multiple_of(((hi * 4 + yi) * 2 + ci) * FEAT, FEAT), FEAT)

    def tsend(hi, yi, rows, dev):
        ref = tok.at[rows, tcols(hi, yi, c)]
        return send(ref, ref, dev)

    tq = {}

    def t_own():
        def own(rows, dev):
            return send(tok_ref.at[rows, :], tok.at[rows, tcols(xh, y, c)], dev)

        tq["h"] = own(ALL, dev_h)
        tq["pa"], tq["mb"] = own(TA, dev_yp), own(TB, dev_ym)
        tq["pb"], tq["ma"] = own(TB, dev_yp), own(TA, dev_ym)
        tq["c0"] = own(ALL, dev_c)

    def t_partner():
        got(tq["h"])
        tq["hpa"], tq["hmb"] = tsend(oh, y, TA, dev_yp), tsend(oh, y, TB, dev_ym)
        tq["hpb"], tq["hma"] = tsend(oh, y, TB, dev_yp), tsend(oh, y, TA, dev_ym)
        tq["c1"] = tsend(oh, y, ALL, dev_c)

    def t_forward_own():
        got(tq["pa"])
        tq["fa"] = tsend(xh, ym, TA, dev_yp)
        got(tq["mb"])
        tq["fb"] = tsend(xh, yp, TB, dev_ym)

    def t_share_own():
        got(tq["pb"])
        tq["c2"] = tsend(xh, ym, ALL, dev_c)
        got(tq["ma"])
        tq["c3"] = tsend(xh, yp, ALL, dev_c)

    def t_forward_partner():
        got(tq["hpa"])
        tq["hfa"] = tsend(oh, ym, TA, dev_yp)
        got(tq["hmb"])
        tq["hfb"] = tsend(oh, yp, TB, dev_ym)
        got(tq["hpb"])
        tq["c4"] = tsend(oh, ym, ALL, dev_c)
        got(tq["hma"])
        tq["c5"] = tsend(oh, yp, ALL, dev_c)

    def t_last_own():
        got(tq["fa"], tq["fb"])
        tq["c6"] = tsend(xh, y2, ALL, dev_c)

    def t_last():
        got(tq["hfa"], tq["hfb"])
        tq["c7"] = tsend(oh, y2, ALL, dev_c)

    def t_done():
        got(*(tq["c%d" % i] for i in range(8)))

    dq = {}

    def hidden(h, r):
        cols = pl.ds(h * BLK, BLK)

        def tile(i, carry):
            at = pl.ds(pl.multiple_of(i * 256, 256), 256)
            hid[...] = dot(tok[at, :], wf[:, cols])

            def slope(j, inner):
                small = pl.ds(pl.multiple_of(j * 16, 16), 16)
                big = pl.ds(pl.multiple_of(i * 256 + j * 16, 16), 16)
                cot = hg[big, cols].astype(F32)
                hg[big, cols] = (cot * gelu_slope(hid[small, :])).astype(BF16)
                return inner

            lax.fori_loop(0, 16, slope, 0, unroll=4)
            return carry

        lax.fori_loop(2 * r, 2 * r + 2, tile, 0)

    def gradient(h):
        cols = pl.ds(h * BLK, BLK)
        for i in range(4):
            at = pl.ds(i * 256, 256)
            hgt[:, at] = hg[at, cols].T

        def block(d, carry):
            at = pl.ds(pl.multiple_of(d * BLK, BLK), BLK)
            part[h, d] = (dot(hgt[...], tok[:, at]) * grad_scale).astype(BF16)
            return carry

        lax.fori_loop(0, 8, block, 0, unroll=8)

    def wide_dot(rows, g):
        at = pl.ds(pl.multiple_of(g * FEAT, FEAT), FEAT)
        return lax.dot_general(
            hg[rows, :], wf[at, :], (((1,), (1,)), ((), ())), preferred_element_type=F32
        )

    def input_other(r):
        rows = pl.ds(r * (TOK // 2), TOK // 2)

        def block(t, carry):
            dout[t, rows, :] = wide_dot(rows, t * 2 + oc).astype(BF16)
            return carry

        lax.fori_loop(0, 8, block, 0, unroll=8)
        dq["c", r] = send(dout.at[:, rows, :], sib.at[:, rows, :], dev_c)

    def input_own(r):
        got(dq["c", r])
        rows = pl.ds(r * (TOK // 2), TOK // 2)

        def block(t, carry):
            mine = wide_dot(rows, t * 2 + c) + sib[t, rows, :].astype(F32)
            sib[t, rows, :] = mine.astype(BF16)
            return carry

        lax.fori_loop(0, 8, block, 0, unroll=8)

    def ppart(h, zi, li, rows):
        return part.at[h, zi * 2 + li, pl.ds(rows[0], rows[1]), :]

    gstate = [dict(), dict()]
    OTHER, OWN = 0, 1
    DN, UP = 0, 1

    def g_start(h):
        q = gstate[h]
        for zi, name in ((u2, "rz2"), (up, "rzp"), (um, "rzm"), (z, "rz0")):
            q[name] = send(ppart(h, zi, m, ZZ), rz.at[h, zi], dev_x)
        for side, li in ((OTHER, m), (OWN, l)):
            q["1p", side] = send(ppart(h, u2, li, XA), s1.at[h, UP, side], dev_zp)
            q["1m", side] = send(ppart(h, u2, li, XB), s1.at[h, DN, side], dev_zm)
        for side, li in ((OTHER, m), (OWN, l)):
            q["2pb", side] = send(ppart(h, up, li, XB), s2.at[h, UP, side, 1], dev_zp)
            q["2ma", side] = send(ppart(h, um, li, XA), s2.at[h, DN, side, 0], dev_zm)

    def g_second(h):
        q = gstate[h]
        for side, li in ((OTHER, m), (OWN, l)):
            got(q["1p", side])
            mine = ppart(h, up, li, XA)
            add_rows(mine, (mine, s1.at[h, UP, side]), XA[1])
            q["2pa", side] = send(mine, s2.at[h, UP, side, 0], dev_zp)
            got(q["1m", side])
            mine = ppart(h, um, li, XB)
            add_rows(mine, (mine, s1.at[h, DN, side]), XB[1])
            q["2mb", side] = send(mine, s2.at[h, DN, side, 1], dev_zm)

    def g_middle(h):
        q = gstate[h]
        for zi, name in ((u2, "rz2"), (up, "rzp"), (um, "rzm"), (z, "rz0")):
            got(q[name])
            mine = ppart(h, zi, l, ZZ)
            add_rows(mine, (mine, rz.at[h, zi]), ZZ[1])
        q["z1p"] = send(ppart(h, u2, l, ZA), s1z.at[h, UP], dev_zp)
        q["z1m"] = send(ppart(h, u2, l, ZB), s1z.at[h, DN], dev_zm)
        q["z2pb"] = send(ppart(h, up, l, ZB), s2z.at[h, UP, 1], dev_zp)
        q["z2ma"] = send(ppart(h, um, l, ZA), s2z.at[h, DN, 0], dev_zm)

    def g_middle_second(h):
        q = gstate[h]
        got(q["z1p"])
        mine = ppart(h, up, l, ZA)
        add_rows(mine, (mine, s1z.at[h, UP]), ZA[1])
        q["z2pa"] = send(mine, s2z.at[h, UP, 0], dev_zp)
        got(q["z1m"])
        mine = ppart(h, um, l, ZB)
        add_rows(mine, (mine, s1z.at[h, DN]), ZB[1])
        q["z2mb"] = send(mine, s2z.at[h, DN, 1], dev_zm)

    def g_cross(h):
        q = gstate[h]
        for k, rows, name in ((0, XA, "a"), (1, XB, "b")):
            got(q["2p" + name, OTHER], q["2m" + name, OTHER])
            mine = ppart(h, z, m, rows)
            add_rows(mine, (mine, s2.at[h, UP, OTHER, k], s2.at[h, DN, OTHER, k]), rows[1])
            q["x" + name] = send(mine, rx.at[h, k], dev_x)

    def g_final(h):
        q = gstate[h]
        out = gt0 if h == 0 else gt_ref
        for k, rows, name in ((0, ZA, "a"), (1, ZB, "b")):
            got(q["z2p" + name], q["z2m" + name])
            add_rows(
                out.at[pl.ds(rows[0], rows[1]), :],
                (ppart(h, z, l, rows), s2z.at[h, UP, k], s2z.at[h, DN, k]),
                rows[1],
            )
        for k, rows, name in ((0, XA, "a"), (1, XB, "b")):
            got(q["2p" + name, OWN], q["2m" + name, OWN], q["x" + name])
            add_rows(
                out.at[pl.ds(rows[0], rows[1]), :],
                (ppart(h, z, l, rows), s2.at[h, UP, OWN, k], s2.at[h, DN, OWN, k], rx.at[h, k]),
                rows[1],
            )

    def dpart(hi, yi, ci, rows):
        return sib.at[hi * 4 + yi, rows, :]

    sides = ((OTHER, oh), (OWN, xh))

    def d_first(r):
        for side, hi in sides:
            if r == 0:
                dq["1p", side] = send(dpart(hi, y2, c, TA), t1.at[UP, side], dev_yp)
                dq["2ma", side] = send(dpart(hi, ym, c, TA), t2.at[DN, side, 0], dev_ym)
            else:
                dq["1m", side] = send(dpart(hi, y2, c, TB), t1.at[DN, side], dev_ym)
                dq["2pb", side] = send(dpart(hi, yp, c, TB), t2.at[UP, side, 1], dev_yp)

    def d_second():
        for side, hi in sides:
            got(dq["1p", side])
            mine = dpart(hi, yp, c, TA)
            add_rows(mine, (mine, t1.at[UP, side]), TOK // 2)
            dq["2pa", side] = send(mine, t2.at[UP, side, 0], dev_yp)
            got(dq["1m", side])
            mine = dpart(hi, ym, c, TB)
            add_rows(mine, (mine, t1.at[DN, side]), TOK // 2)
            dq["2mb", side] = send(mine, t2.at[DN, side, 1], dev_ym)

    def d_cross():
        for k, rows, name in ((0, TA, "a"), (1, TB, "b")):
            got(dq["2p" + name, OTHER], dq["2m" + name, OTHER])
            mine = dpart(oh, y, c, rows)
            add_rows(mine, (mine, t2.at[UP, OTHER, k], t2.at[DN, OTHER, k]), TOK // 2)
            dq["x" + name] = send(mine, tx.at[k], dev_h)

    def d_final():
        for k, rows, name in ((0, TA, "a"), (1, TB, "b")):
            got(dq["2p" + name, OWN], dq["2m" + name, OWN], dq["x" + name])
            add_rows(
                tg_ref.at[rows, :],
                (dpart(xh, y, c, rows), t2.at[UP, OWN, k], t2.at[DN, OWN, k], tx.at[k]),
                TOK // 2,
            )

    def newton(h):
        for copy in held:
            copy.wait()

        slots = iter(
            [wf.at[pl.ds(i * BLK, BLK), pl.ds(j * BLK, BLK)] for i in range(8) for j in range(2)]
            + [tok.at[pl.ds(0, BLK), pl.ds(j * BLK, BLK)] for j in range(8)]
        )
        gh, gth, lp = next(slots), next(slots), next(slots)
        mh, zs, cr, fo, tw, tq2, tc, tf, root = [(next(slots), next(slots)) for _ in range(9)]
        pieces = [pl.ds(i * 256, 256) for i in range(2)]
        ids = lax.broadcasted_iota(jnp.int32, (256, BLK), 0)
        across = lax.broadcasted_iota(jnp.int32, (256, BLK), 1)
        eyes = [jnp.where(ids + i * 256 == across, 1.0, 0.0).astype(F32) for i in range(2)]
        share = (1.0 - decay_rate) / BLK

        gth[...] = gt0[...].astype(BF16)
        gh[...] = gt0[...].T.astype(BF16)
        trace, norm = [0.0, 0.0], [0.0, 0.0]
        for i, rows in enumerate(pieces):
            for side, (a, b) in enumerate(((gh, gth), (gth, gh))):
                new = decay_rate * stat[side, rows, :] + share * dot(a[rows, :], b[...])
                stat[side, rows, :] = new
                trace[side] += total_of(new * eyes[i])
                norm[side] += total_of(new * new)
        for side, out in enumerate((lnew_ref, rnew_ref)):
            back = pltpu.make_async_copy(stat.at[side], out, ls.at[5 + side])
            back.start()
            backs.append(back)
        scale = [None, None]
        for side in range(2):
            ridge = ridge_share * trace[side] / BLK
            full = norm[side] + 2.0 * ridge * trace[side] + BLK * ridge * ridge
            scale[side] = jnp.sqrt(full) / 4.0
            for i, rows in enumerate(pieces):
                first = (stat[side, rows, :] + ridge * eyes[i]) / scale[side]
                work[side, rows, :] = first
                mh[side][rows, :] = first.astype(BF16)
        for i, rows in enumerate(pieces):
            for side in range(2):
                first = work[side, rows, :]
                square = dot(mh[side][rows, :], mh[side][...])
                zs[side][rows, :] = (1.5625 * eyes[i] - 0.625 * first + 0.0625 * square).astype(BF16)
                cr[side][rows, :] = (1.25 * first - 0.25 * square).astype(BF16)
        for rows in pieces:
            for side in range(2):
                fo[side][rows, :] = dot(zs[side][rows, :], zs[side][...]).astype(BF16)
        for i, rows in enumerate(pieces):
            for side in range(2):
                two = (
                    1.5625 * eyes[i]
                    - 0.3125 * work[side, rows, :]
                    - 0.25 * dot(fo[side][rows, :], cr[side][...])
                )
                work[side, rows, :] = two
                tw[side][rows, :] = two.astype(BF16)
        for rows in pieces:
            for side in range(2):
                tq2[side][rows, :] = dot(tw[side][rows, :], tw[side][...]).astype(BF16)
                tc[side][rows, :] = dot(tw[side][rows, :], mh[side][...]).astype(BF16)
        for rows in pieces:
            for side in range(2):
                tf[side][rows, :] = dot(tq2[side][rows, :], tq2[side][...]).astype(BF16)
        for rows in pieces:
            for side in range(2):
                three = 1.25 * work[side, rows, :] - 0.25 * dot(tf[side][rows, :], tc[side][...])
                root[side][rows, :] = (lax.rsqrt(jnp.sqrt(scale[side])) * three).astype(BF16)
        for rows in pieces:
            lp[rows, :] = dot(root[0][rows, :], gh[...]).astype(BF16)
        raw_sum, grad_sum = 0.0, 0.0
        for rows in pieces:
            raw = dot(lp[rows, :], root[1][...])
            work[0, rows, :] = raw
            raw_sum += total_of(raw * raw)
            grad_sum += total_of(gt0[rows, :] * gt0[rows, :])
        size = float(BLK * BLK)
        ratio = jnp.sqrt(grad_sum / size) / jnp.sqrt(raw_sum / size + epsilon)
        for rows in pieces:
            up_ref[rows, :] = (work[0, rows, :] * ratio).astype(BF16)

    local = [
        pltpu.make_async_copy(w_ref, wf.at[rows_of(z, l, (0, BLK)), :], ls.at[0]),
        pltpu.make_async_copy(tok_ref, tok.at[:, tcols(xh, y, c)], ls.at[1]),
        pltpu.make_async_copy(cot_ref, hg, ls.at[2]),
    ]
    held = [
        pltpu.make_async_copy(left_ref.at[0, 0], stat.at[0], ls.at[3]),
        pltpu.make_async_copy(right_ref.at[0, 0], stat.at[1], ls.at[4]),
    ]
    backs = []
    w_own(1, False)
    t_own()
    w_own(0, True)
    t_forward_own()
    for copy in local + held:
        copy.start()
    w_own(1, True)
    w_forward_own(0)
    w_own(0, False)
    t_last_own()
    w_partner(0)
    w_last(0)
    w_forward_own(1)
    t_partner()
    w_cross(0)
    w_forward_partner(0)
    w_partner(1)
    t_forward_partner()
    t_last()
    t_share_own()
    w_last(1)
    t_done()
    w_done(0)
    w_cross(1)
    for copy in local:
        copy.wait()
    hidden(0, 0)
    w_forward_partner(1)
    hidden(0, 1)
    gradient(0)
    g_start(0)
    w_done(1)
    hidden(1, 0)
    input_other(0)
    hidden(1, 1)
    input_other(1)
    input_own(0)
    d_first(0)
    g_second(0)
    release()
    gradient(1)
    g_middle(0)
    g_start(1)
    input_own(1)
    d_first(1)
    g_cross(0)
    d_second()
    g_middle_second(0)
    g_second(1)
    d_cross()
    g_final(0)
    g_middle(1)
    g_cross(1)
    newton(0)
    g_middle_second(1)
    d_final()
    g_final(1)
    for copy in backs:
        copy.wait()
    release()


def exchange(tokens, weight, cotangent, left_stats, right_stats):
    any_spec = pl.BlockSpec(memory_space=pl.ANY)
    vmem_spec = pl.BlockSpec(memory_space=pltpu.VMEM)
    dma = pltpu.SemaphoreType.DMA
    square = jax.ShapeDtypeStruct((BLK, BLK), F32)
    return pl.pallas_call(
        exchange_kernel,
        out_shape=(
            jax.ShapeDtypeStruct((TOK, FEAT), BF16),
            square,
            jax.ShapeDtypeStruct((BLK, BLK), BF16),
            square,
            square,
        ),
        in_specs=[any_spec] * 5,
        out_specs=(vmem_spec, vmem_spec, vmem_spec, any_spec, any_spec),
        scratch_shapes=[
            pltpu.VMEM((D, COLS), BF16),
            pltpu.VMEM((TOK, D), BF16),
            pltpu.VMEM((TOK, COLS), BF16),
            pltpu.VMEM((BLK, TOK), BF16),
            pltpu.VMEM((256, BLK), F32),
            pltpu.VMEM((2, 8, BLK, BLK), BF16),
            pltpu.VMEM((8, TOK, FEAT), BF16),
            pltpu.VMEM((2, 2, 2, XA[1], BLK), BF16),
            pltpu.VMEM((2, 2, ZA[1], BLK), BF16),
            pltpu.VMEM((2, 2, 2, 2, XA[1], BLK), BF16),
            pltpu.VMEM((2, 2, 2, ZA[1], BLK), BF16),
            pltpu.VMEM((2, 4, ZZ[1], BLK), BF16),
            pltpu.VMEM((2, 2, XA[1], BLK), BF16),
            pltpu.VMEM((8, TOK, FEAT), BF16),
            pltpu.VMEM((2, 2, TOK // 2, FEAT), BF16),
            pltpu.VMEM((2, 2, 2, TOK // 2, FEAT), BF16),
            pltpu.VMEM((2, TOK // 2, FEAT), BF16),
            pltpu.VMEM((BLK, BLK), F32),
            pltpu.VMEM((2, BLK, BLK), F32),
            pltpu.VMEM((2, BLK, BLK), F32),
            dma((N_SEND,)),
            dma((N_RECV,)),
            dma((7,)),
        ],
        compiler_params=pltpu.CompilerParams(
            collective_id=0, has_side_effects=True, vmem_limit_bytes=62 * 2**20
        ),
        cost_estimate=pl.CostEstimate(
            flops=6 * TOK * D * COLS, bytes_accessed=2**24, transcendentals=2 * TOK * COLS
        ),
        name="exchange",
    )(tokens, weight, cotangent, left_stats, right_stats)


def precondition_kernel(
    gt_ref, left_ref, right_ref, tg_ref, up_ref, lnew_ref, rnew_ref,
    tg_out, update_ref, left_out, right_out,
    up, lnew, rnew, tg_held, up_held, l_held, r_held, sems,
):
    def move(i, source, target):
        copy = pltpu.make_async_copy(source, target, sems.at[i])
        copy.start()
        return copy

    holds = (
        (tg_ref, tg_held, tg_out),
        (up_ref, up_held, update_ref.at[:, pl.ds(0, BLK)]),
        (lnew_ref, l_held, left_out.at[0, 0]),
        (rnew_ref, r_held, right_out.at[0, 0]),
    )
    olds = [
        move(11, left_ref.at[0, 1], lnew),
        move(12, right_ref.at[0, 1], rnew),
    ]
    arriving = [move(i, source, held) for i, (source, held, _) in enumerate(holds)]
    passed = []
    gt = gt_ref[...]
    grad = gt.T
    gth, gh = gt.astype(BF16), grad.astype(BF16)
    rows = lax.broadcasted_iota(jnp.int32, (BLK, BLK), 0)
    cols = lax.broadcasted_iota(jnp.int32, (BLK, BLK), 1)
    eye = jnp.where(rows == cols, 1.0, 0.0).astype(F32)
    share = (1.0 - decay_rate) / BLK
    left, right = share * dot(gh, gth), share * dot(gth, gh)
    for copy in olds:
        copy.wait()
    left = decay_rate * lnew[...] + left
    right = decay_rate * rnew[...] + right
    lnew[...] = left
    rnew[...] = right
    for i, (copy, (_, held, target)) in enumerate(zip(arriving, holds)):
        copy.wait()
        passed.append(move(7 + i, held, target))
    passed.append(move(4, lnew, left_out.at[0, 1]))
    passed.append(move(5, rnew, right_out.at[0, 1]))

    def each(function, *lists):
        return [function(*items) for items in zip(*lists)]

    def start(stat):
        trace = total_of(stat * eye)
        regular = stat + (ridge_share * trace / BLK) * eye
        scale = jnp.sqrt(total_of(regular * regular)) / 4.0
        return regular / scale, scale

    begun = each(start, (left, right))
    first = [b[0] for b in begun]
    scales = [b[1] for b in begun]
    firsth = each(lambda a: a.astype(BF16), first)
    square = each(dot, firsth, firsth)
    zero_sq = each(
        lambda a, q: (1.5625 * eye - 0.625 * a + 0.0625 * q).astype(BF16), first, square
    )
    crossed = each(lambda a, q: (1.25 * a - 0.25 * q).astype(BF16), first, square)
    fourth = each(lambda a: dot(a, a).astype(BF16), zero_sq)
    two = each(
        lambda a, f, x: 1.5625 * eye - 0.3125 * a - 0.25 * dot(f, x), first, fourth, crossed
    )
    twoh = each(lambda a: a.astype(BF16), two)
    two_sq = each(lambda a: dot(a, a).astype(BF16), twoh)
    two_crossed = each(lambda a, f: dot(a, f).astype(BF16), twoh, firsth)
    two_fourth = each(lambda a: dot(a, a).astype(BF16), two_sq)
    roots = each(
        lambda a, f, x, s: (
            lax.rsqrt(jnp.sqrt(s)) * (1.25 * a - 0.25 * dot(f, x))
        ).astype(BF16),
        two, two_fourth, two_crossed, scales,
    )
    left_part = dot(roots[0], gh).astype(BF16)
    raw = dot(left_part, roots[1])
    size = float(BLK * BLK)
    grad_rms = jnp.sqrt(total_of(gt * gt) / size)
    raw_rms = jnp.sqrt(total_of(raw * raw) / size + epsilon)
    up[...] = (raw * (grad_rms / raw_rms)).astype(BF16)
    passed.append(move(6, up, update_ref.at[:, pl.ds(BLK, BLK)]))
    for copy in passed:
        copy.wait()


def precondition(gt, left_stats, right_stats, tokens_grad, up, left_new, right_new):
    any_spec = pl.BlockSpec(memory_space=pl.ANY)
    return pl.pallas_call(
        precondition_kernel,
        grid=(1,),
        out_shape=(
            jax.ShapeDtypeStruct((TOK, FEAT), BF16),
            jax.ShapeDtypeStruct((BLK, COLS), BF16),
            jax.ShapeDtypeStruct(left_stats.shape, F32),
            jax.ShapeDtypeStruct(right_stats.shape, F32),
        ),
        in_specs=[pl.BlockSpec((BLK, BLK), lambda i: (0, 0))] + [any_spec] * 6,
        out_specs=(any_spec,) * 4,
        scratch_shapes=[
            pltpu.VMEM((BLK, BLK), BF16),
            pltpu.VMEM((BLK, BLK), F32),
            pltpu.VMEM((BLK, BLK), F32),
            pltpu.VMEM((TOK, FEAT), BF16),
            pltpu.VMEM((BLK, BLK), BF16),
            pltpu.VMEM((BLK, BLK), F32),
            pltpu.VMEM((BLK, BLK), F32),
            pltpu.SemaphoreType.DMA((13,)),
        ],
        compiler_params=pltpu.CompilerParams(vmem_limit_bytes=62 * 2**20),
        name="precondition",
    )(gt, left_stats, right_stats, tokens_grad, up, left_new, right_new)


def shards(tokens, weight, cotangent, left_stats, right_stats):
    tokens_grad, gt, up, left_half, right_half = exchange(
        tokens, weight, cotangent, left_stats, right_stats
    )
    return precondition(gt, left_stats, right_stats, tokens_grad, up, left_half, right_half)


def solution(mesh):
    two = P("dp", ("tensor", "pre"))
    four = P("dp", ("tensor", "pre"), None, None)
    return jax.shard_map(
        shards,
        mesh=mesh,
        in_specs=(two, two, two, four, four),
        out_specs=(two, two, four, four),
        check_vma=False,
    )
```

```python
import jax
import jax.numpy as jnp
from jax import lax
from jax.experimental import pallas as pl
from jax.experimental.pallas import tpu as pltpu
from jax.sharding import PartitionSpec as P

MESH = pl.DeviceIdType.MESH
F32 = jnp.float32
BF16 = jnp.bfloat16

TOK = 1024
D = 4096
BLK = 512
COLS = 1024
FEAT = 256

decay_rate = 0.5
ridge_share = 0.05
epsilon = 1e-06
grad_scale = float(8192) ** (-0.5)

XA = (0, 176)
ZA = (176, 80)
ZB = (256, 80)
XB = (336, 176)
ZZ = (176, 160)
HA = (0, 256)
HB = (256, 256)
N_SEND = 86
N_RECV = 126


def dot(a, b):
    return jnp.dot(a, b, preferred_element_type=F32)


def gelu_slope(values):
    return (
        0.5 * (1.0 + lax.erf(values * 0.7071067811865476))
        + values * jnp.exp(-0.5 * values * values) * 0.3989422804014327
    )


def add_rows(dst, sources, rows, chunk=16):
    def body(i, carry):
        at = pl.ds(pl.multiple_of(i * chunk, chunk), chunk)
        total = sources[0][at, :].astype(F32)
        for source in sources[1:]:
            total = total + source[at, :].astype(F32)
        dst[at, :] = total.astype(dst.dtype)
        return carry

    lax.fori_loop(0, rows // chunk, body, 0)


def total_of(values):
    return jnp.sum(jnp.sum(values, axis=1, keepdims=True), axis=0, keepdims=True)


def exchange_kernel(
    tok_ref, w_ref, cot_ref, left_ref, right_ref, tg_ref, gt_ref, up_ref, lnew_ref, rnew_ref,
    wf, tok, hg, hgt, hid, part, dout,
    s1, s1z, s2, s2z, rz, rx, sib, t1, t2, tx, gt0, stat, work,
    ss, rs, ls,
):
    dp = lax.axis_index("dp")
    tn = lax.axis_index("tensor")
    c = lax.axis_index("pre")
    z, l = lax.div(dp, 2), lax.rem(dp, 2)
    xh, y = lax.div(tn, 4), lax.rem(tn, 4)
    m = 1 - l
    up, um, u2 = lax.rem(z + 1, 4), lax.rem(z + 3, 4), lax.rem(z + 2, 4)
    yp, ym, y2 = lax.rem(y + 1, 4), lax.rem(y + 3, 4), lax.rem(y + 2, 4)
    oh, oc = 1 - xh, 1 - c
    dev_zp, dev_zm = (up * 2 + l, tn, c), (um * 2 + l, tn, c)
    dev_x = (z * 2 + m, tn, c)
    dev_yp, dev_ym = (dp, xh * 4 + yp, c), (dp, xh * 4 + ym, c)
    dev_h = (dp, oh * 4 + y, c)
    dev_c = (dp, tn, oc)

    barrier = pltpu.get_barrier_semaphore()
    for dev in (dev_zp, dev_zm, dev_x, dev_yp, dev_ym, dev_h, dev_c):
        pl.semaphore_signal(barrier, inc=1, device_id=dev, device_id_type=MESH)
    pl.semaphore_wait(barrier, 7)

    copies, pending = [], []
    unused = list(range(N_SEND))

    def send(src, dst, dev):
        k = unused.pop(0)
        copy = pltpu.make_async_remote_copy(
            src_ref=src, dst_ref=dst, send_sem=ss.at[k], recv_sem=rs.at[len(copies)],
            device_id=dev, device_id_type=MESH,
        )
        copy.start()
        copies.append(copy)
        pending.append((copy, k))
        return copy

    def release():
        for copy, k in pending:
            copy.wait_send()
            unused.append(k)
        pending.clear()

    def got(*several):
        for copy in several:
            copy.wait_recv()

    def rows_of(zi, li, rows):
        return pl.ds(pl.multiple_of((zi * 2 + li) * BLK + rows[0], 16), rows[1])

    def wpart(zi, li, rows, h):
        return wf.at[rows_of(zi, li, rows), pl.ds(h * BLK, BLK)]

    def wsend(zi, li, rows, h, dev):
        ref = wpart(zi, li, rows, h)
        return send(ref, ref, dev)

    wstate = [dict(), dict()]

    def w_own(h, first):
        q = wstate[h]

        def own(rows, dev):
            return send(
                w_ref.at[pl.ds(rows[0], rows[1]), pl.ds(h * BLK, BLK)],
                wpart(z, l, rows, h), dev,
            )

        if first:
            q["pa"], q["mb"] = own(HA, dev_zp), own(HB, dev_zm)
            q["xa"], q["xb"] = own(XA, dev_x), own(XB, dev_x)
        else:
            q["pb"], q["ma"] = own(HB, dev_zp), own(HA, dev_zm)
            q["xz"] = own(ZZ, dev_x)

    def w_partner(h):
        q = wstate[h]
        got(q["xa"])
        q["ppa"] = wsend(z, m, XA, h, dev_zp)
        got(q["xb"])
        q["pmb"] = wsend(z, m, XB, h, dev_zm)
        q["ppb"] = wsend(z, m, XB, h, dev_zp)
        q["pma"] = wsend(z, m, XA, h, dev_zm)

    def w_forward_own(h):
        q = wstate[h]
        got(q["pa"])
        q["fa"] = wsend(um, l, HA, h, dev_zp)
        got(q["mb"])
        q["fb"] = wsend(up, l, HB, h, dev_zm)

    def w_cross(h):
        q = wstate[h]
        got(q["pb"])
        q["xzm"] = wsend(um, l, ZZ, h, dev_x)
        got(q["ma"])
        q["xzp"] = wsend(up, l, ZZ, h, dev_x)

    def w_forward_partner(h):
        q = wstate[h]
        got(q["ppa"])
        q["fpa"] = wsend(um, m, XA, h, dev_zp)
        got(q["pmb"])
        q["fpb"] = wsend(up, m, XB, h, dev_zm)

    def w_last(h):
        q = wstate[h]
        got(q["fa"])
        q["x2a"] = wsend(u2, l, ZA, h, dev_x)
        got(q["fb"])
        q["x2b"] = wsend(u2, l, ZB, h, dev_x)

    def w_done(h):
        q = wstate[h]
        got(*(q[k] for k in ("xz", "ppb", "pma", "xzm", "xzp", "fpa", "fpb", "x2a", "x2b")))

    TA, TB = pl.ds(0, TOK // 2), pl.ds(TOK // 2, TOK // 2)
    ALL = pl.ds(0, TOK)

    def tcols(hi, yi, ci):
        return pl.ds(pl.multiple_of(((hi * 4 + yi) * 2 + ci) * FEAT, FEAT), FEAT)

    def tsend(hi, yi, rows, dev):
        ref = tok.at[rows, tcols(hi, yi, c)]
        return send(ref, ref, dev)

    tq = {}

    def t_own():
        def own(rows, dev):
            return send(tok_ref.at[rows, :], tok.at[rows, tcols(xh, y, c)], dev)

        tq["h"] = own(ALL, dev_h)
        tq["pa"], tq["mb"] = own(TA, dev_yp), own(TB, dev_ym)
        tq["pb"], tq["ma"] = own(TB, dev_yp), own(TA, dev_ym)
        tq["c0"] = own(ALL, dev_c)

    def t_partner():
        got(tq["h"])
        tq["hpa"], tq["hmb"] = tsend(oh, y, TA, dev_yp), tsend(oh, y, TB, dev_ym)
        tq["hpb"], tq["hma"] = tsend(oh, y, TB, dev_yp), tsend(oh, y, TA, dev_ym)
        tq["c1"] = tsend(oh, y, ALL, dev_c)

    def t_forward_own():
        got(tq["pa"])
        tq["fa"] = tsend(xh, ym, TA, dev_yp)
        got(tq["mb"])
        tq["fb"] = tsend(xh, yp, TB, dev_ym)

    def t_share_own():
        got(tq["pb"])
        tq["c2"] = tsend(xh, ym, ALL, dev_c)
        got(tq["ma"])
        tq["c3"] = tsend(xh, yp, ALL, dev_c)

    def t_forward_partner():
        got(tq["hpa"])
        tq["hfa"] = tsend(oh, ym, TA, dev_yp)
        got(tq["hmb"])
        tq["hfb"] = tsend(oh, yp, TB, dev_ym)
        got(tq["hpb"])
        tq["c4"] = tsend(oh, ym, ALL, dev_c)
        got(tq["hma"])
        tq["c5"] = tsend(oh, yp, ALL, dev_c)

    def t_last_own():
        got(tq["fa"], tq["fb"])
        tq["c6"] = tsend(xh, y2, ALL, dev_c)

    def t_last():
        got(tq["hfa"], tq["hfb"])
        tq["c7"] = tsend(oh, y2, ALL, dev_c)

    def t_done():
        got(*(tq["c%d" % i] for i in range(8)))

    dq = {}

    def hidden(h, r):
        cols = pl.ds(h * BLK, BLK)

        def tile(i, carry):
            at = pl.ds(pl.multiple_of(i * 256, 256), 256)
            hid[...] = dot(tok[at, :], wf[:, cols])

            def slope(j, inner):
                small = pl.ds(pl.multiple_of(j * 16, 16), 16)
                big = pl.ds(pl.multiple_of(i * 256 + j * 16, 16), 16)
                cot = hg[big, cols].astype(F32)
                hg[big, cols] = (cot * gelu_slope(hid[small, :])).astype(BF16)
                return inner

            lax.fori_loop(0, 16, slope, 0, unroll=4)
            return carry

        lax.fori_loop(2 * r, 2 * r + 2, tile, 0)

    def gradient(h):
        cols = pl.ds(h * BLK, BLK)
        for i in range(4):
            at = pl.ds(i * 256, 256)
            hgt[:, at] = hg[at, cols].T

        def block(d, carry):
            at = pl.ds(pl.multiple_of(d * BLK, BLK), BLK)
            part[h, d] = (dot(hgt[...], tok[:, at]) * grad_scale).astype(BF16)
            return carry

        lax.fori_loop(0, 8, block, 0, unroll=8)

    def wide_dot(rows, g):
        at = pl.ds(pl.multiple_of(g * FEAT, FEAT), FEAT)
        return lax.dot_general(
            hg[rows, :], wf[at, :], (((1,), (1,)), ((), ())), preferred_element_type=F32
        )

    def input_other(r):
        rows = pl.ds(r * (TOK // 2), TOK // 2)

        def block(t, carry):
            dout[t, rows, :] = wide_dot(rows, t * 2 + oc).astype(BF16)
            return carry

        lax.fori_loop(0, 8, block, 0, unroll=8)
        dq["c", r] = send(dout.at[:, rows, :], sib.at[:, rows, :], dev_c)

    def input_own(r):
        got(dq["c", r])
        rows = pl.ds(r * (TOK // 2), TOK // 2)

        def block(t, carry):
            mine = wide_dot(rows, t * 2 + c) + sib[t, rows, :].astype(F32)
            sib[t, rows, :] = mine.astype(BF16)
            return carry

        lax.fori_loop(0, 8, block, 0, unroll=8)

    def ppart(h, zi, li, rows):
        return part.at[h, zi * 2 + li, pl.ds(rows[0], rows[1]), :]

    gstate = [dict(), dict()]
    OTHER, OWN = 0, 1
    DN, UP = 0, 1

    def g_start(h):
        q = gstate[h]
        for zi, name in ((u2, "rz2"), (up, "rzp"), (um, "rzm"), (z, "rz0")):
            q[name] = send(ppart(h, zi, m, ZZ), rz.at[h, zi], dev_x)
        for side, li in ((OTHER, m), (OWN, l)):
            q["1p", side] = send(ppart(h, u2, li, XA), s1.at[h, UP, side], dev_zp)
            q["1m", side] = send(ppart(h, u2, li, XB), s1.at[h, DN, side], dev_zm)
        for side, li in ((OTHER, m), (OWN, l)):
            q["2pb", side] = send(ppart(h, up, li, XB), s2.at[h, UP, side, 1], dev_zp)
            q["2ma", side] = send(ppart(h, um, li, XA), s2.at[h, DN, side, 0], dev_zm)

    def g_second(h):
        q = gstate[h]
        for side, li in ((OTHER, m), (OWN, l)):
            got(q["1p", side])
            mine = ppart(h, up, li, XA)
            add_rows(mine, (mine, s1.at[h, UP, side]), XA[1])
            q["2pa", side] = send(mine, s2.at[h, UP, side, 0], dev_zp)
            got(q["1m", side])
            mine = ppart(h, um, li, XB)
            add_rows(mine, (mine, s1.at[h, DN, side]), XB[1])
            q["2mb", side] = send(mine, s2.at[h, DN, side, 1], dev_zm)

    def g_middle(h):
        q = gstate[h]
        for zi, name in ((u2, "rz2"), (up, "rzp"), (um, "rzm"), (z, "rz0")):
            got(q[name])
            mine = ppart(h, zi, l, ZZ)
            add_rows(mine, (mine, rz.at[h, zi]), ZZ[1])
        q["z1p"] = send(ppart(h, u2, l, ZA), s1z.at[h, UP], dev_zp)
        q["z1m"] = send(ppart(h, u2, l, ZB), s1z.at[h, DN], dev_zm)
        q["z2pb"] = send(ppart(h, up, l, ZB), s2z.at[h, UP, 1], dev_zp)
        q["z2ma"] = send(ppart(h, um, l, ZA), s2z.at[h, DN, 0], dev_zm)

    def g_middle_second(h):
        q = gstate[h]
        got(q["z1p"])
        mine = ppart(h, up, l, ZA)
        add_rows(mine, (mine, s1z.at[h, UP]), ZA[1])
        q["z2pa"] = send(mine, s2z.at[h, UP, 0], dev_zp)
        got(q["z1m"])
        mine = ppart(h, um, l, ZB)
        add_rows(mine, (mine, s1z.at[h, DN]), ZB[1])
        q["z2mb"] = send(mine, s2z.at[h, DN, 1], dev_zm)

    def g_cross(h):
        q = gstate[h]
        for k, rows, name in ((0, XA, "a"), (1, XB, "b")):
            got(q["2p" + name, OTHER], q["2m" + name, OTHER])
            mine = ppart(h, z, m, rows)
            add_rows(mine, (mine, s2.at[h, UP, OTHER, k], s2.at[h, DN, OTHER, k]), rows[1])
            q["x" + name] = send(mine, rx.at[h, k], dev_x)

    def g_final(h):
        q = gstate[h]
        out = gt0 if h == 0 else gt_ref
        for k, rows, name in ((0, ZA, "a"), (1, ZB, "b")):
            got(q["z2p" + name], q["z2m" + name])
            add_rows(
                out.at[pl.ds(rows[0], rows[1]), :],
                (ppart(h, z, l, rows), s2z.at[h, UP, k], s2z.at[h, DN, k]),
                rows[1],
            )
        for k, rows, name in ((0, XA, "a"), (1, XB, "b")):
            got(q["2p" + name, OWN], q["2m" + name, OWN], q["x" + name])
            add_rows(
                out.at[pl.ds(rows[0], rows[1]), :],
                (ppart(h, z, l, rows), s2.at[h, UP, OWN, k], s2.at[h, DN, OWN, k], rx.at[h, k]),
                rows[1],
            )

    def dpart(hi, yi, ci, rows):
        return sib.at[hi * 4 + yi, rows, :]

    sides = ((OTHER, oh), (OWN, xh))

    def d_first(r):
        for side, hi in sides:
            if r == 0:
                dq["1p", side] = send(dpart(hi, y2, c, TA), t1.at[UP, side], dev_yp)
                dq["2ma", side] = send(dpart(hi, ym, c, TA), t2.at[DN, side, 0], dev_ym)
            else:
                dq["1m", side] = send(dpart(hi, y2, c, TB), t1.at[DN, side], dev_ym)
                dq["2pb", side] = send(dpart(hi, yp, c, TB), t2.at[UP, side, 1], dev_yp)

    def d_second():
        for side, hi in sides:
            got(dq["1p", side])
            mine = dpart(hi, yp, c, TA)
            add_rows(mine, (mine, t1.at[UP, side]), TOK // 2)
            dq["2pa", side] = send(mine, t2.at[UP, side, 0], dev_yp)
            got(dq["1m", side])
            mine = dpart(hi, ym, c, TB)
            add_rows(mine, (mine, t1.at[DN, side]), TOK // 2)
            dq["2mb", side] = send(mine, t2.at[DN, side, 1], dev_ym)

    def d_cross():
        for k, rows, name in ((0, TA, "a"), (1, TB, "b")):
            got(dq["2p" + name, OTHER], dq["2m" + name, OTHER])
            mine = dpart(oh, y, c, rows)
            add_rows(mine, (mine, t2.at[UP, OTHER, k], t2.at[DN, OTHER, k]), TOK // 2)
            dq["x" + name] = send(mine, tx.at[k], dev_h)

    def d_final():
        for k, rows, name in ((0, TA, "a"), (1, TB, "b")):
            got(dq["2p" + name, OWN], dq["2m" + name, OWN], dq["x" + name])
            add_rows(
                tg_ref.at[rows, :],
                (dpart(xh, y, c, rows), t2.at[UP, OWN, k], t2.at[DN, OWN, k], tx.at[k]),
                TOK // 2,
            )

    def newton(h):
        for copy in held:
            copy.wait()

        slots = iter(
            [wf.at[pl.ds(i * BLK, BLK), pl.ds(j * BLK, BLK)] for i in range(8) for j in range(2)]
            + [tok.at[pl.ds(0, BLK), pl.ds(j * BLK, BLK)] for j in range(8)]
        )
        gh, gth, lp = next(slots), next(slots), next(slots)
        mh, zs, cr, fo, tw, tq2, tc, tf, root = [(next(slots), next(slots)) for _ in range(9)]
        pieces = [pl.ds(i * 256, 256) for i in range(2)]
        ids = lax.broadcasted_iota(jnp.int32, (256, BLK), 0)
        across = lax.broadcasted_iota(jnp.int32, (256, BLK), 1)
        eyes = [jnp.where(ids + i * 256 == across, 1.0, 0.0).astype(F32) for i in range(2)]
        share = (1.0 - decay_rate) / BLK

        gth[...] = gt0[...].astype(BF16)
        gh[...] = gt0[...].T.astype(BF16)
        trace, norm = [0.0, 0.0], [0.0, 0.0]
        for i, rows in enumerate(pieces):
            for side, (a, b) in enumerate(((gh, gth), (gth, gh))):
                new = decay_rate * stat[side, rows, :] + share * dot(a[rows, :], b[...])
                stat[side, rows, :] = new
                trace[side] += total_of(new * eyes[i])
                norm[side] += total_of(new * new)
        for side, out in enumerate((lnew_ref, rnew_ref)):
            back = pltpu.make_async_copy(stat.at[side], out, ls.at[5 + side])
            back.start()
            backs.append(back)
        scale = [None, None]
        for side in range(2):
            ridge = ridge_share * trace[side] / BLK
            full = norm[side] + 2.0 * ridge * trace[side] + BLK * ridge * ridge
            scale[side] = jnp.sqrt(full) / 4.0
            for i, rows in enumerate(pieces):
                first = (stat[side, rows, :] + ridge * eyes[i]) / scale[side]
                work[side, rows, :] = first
                mh[side][rows, :] = first.astype(BF16)
        for i, rows in enumerate(pieces):
            for side in range(2):
                first = work[side, rows, :]
                square = dot(mh[side][rows, :], mh[side][...])
                zs[side][rows, :] = (1.5625 * eyes[i] - 0.625 * first + 0.0625 * square).astype(BF16)
                cr[side][rows, :] = (1.25 * first - 0.25 * square).astype(BF16)
        for rows in pieces:
            for side in range(2):
                fo[side][rows, :] = dot(zs[side][rows, :], zs[side][...]).astype(BF16)
        for i, rows in enumerate(pieces):
            for side in range(2):
                two = (
                    1.5625 * eyes[i]
                    - 0.3125 * work[side, rows, :]
                    - 0.25 * dot(fo[side][rows, :], cr[side][...])
                )
                work[side, rows, :] = two
                tw[side][rows, :] = two.astype(BF16)
        for rows in pieces:
            for side in range(2):
                tq2[side][rows, :] = dot(tw[side][rows, :], tw[side][...]).astype(BF16)
                tc[side][rows, :] = dot(tw[side][rows, :], mh[side][...]).astype(BF16)
        for rows in pieces:
            for side in range(2):
                tf[side][rows, :] = dot(tq2[side][rows, :], tq2[side][...]).astype(BF16)
        for rows in pieces:
            for side in range(2):
                three = 1.25 * work[side, rows, :] - 0.25 * dot(tf[side][rows, :], tc[side][...])
                root[side][rows, :] = (lax.rsqrt(jnp.sqrt(scale[side])) * three).astype(BF16)
        for rows in pieces:
            lp[rows, :] = dot(root[0][rows, :], gh[...]).astype(BF16)
        raw_sum, grad_sum = 0.0, 0.0
        for rows in pieces:
            raw = dot(lp[rows, :], root[1][...])
            work[0, rows, :] = raw
            raw_sum += total_of(raw * raw)
            grad_sum += total_of(gt0[rows, :] * gt0[rows, :])
        size = float(BLK * BLK)
        ratio = jnp.sqrt(grad_sum / size) / jnp.sqrt(raw_sum / size + epsilon)
        for rows in pieces:
            up_ref[rows, :] = (work[0, rows, :] * ratio).astype(BF16)

    local = [
        pltpu.make_async_copy(w_ref, wf.at[rows_of(z, l, (0, BLK)), :], ls.at[0]),
        pltpu.make_async_copy(tok_ref, tok.at[:, tcols(xh, y, c)], ls.at[1]),
        pltpu.make_async_copy(cot_ref, hg, ls.at[2]),
    ]
    held = [
        pltpu.make_async_copy(left_ref.at[0, 0], stat.at[0], ls.at[3]),
        pltpu.make_async_copy(right_ref.at[0, 0], stat.at[1], ls.at[4]),
    ]
    backs = []
    w_own(1, False)
    t_own()
    w_own(0, True)
    t_forward_own()
    for copy in local + held:
        copy.start()
    w_own(1, True)
    w_forward_own(0)
    w_own(0, False)
    t_last_own()
    w_partner(0)
    w_last(0)
    w_forward_own(1)
    t_partner()
    w_cross(0)
    w_forward_partner(0)
    w_partner(1)
    t_forward_partner()
    t_last()
    t_share_own()
    w_last(1)
    t_done()
    w_done(0)
    w_cross(1)
    for copy in local:
        copy.wait()
    hidden(0, 0)
    w_forward_partner(1)
    hidden(0, 1)
    gradient(0)
    g_start(0)
    w_done(1)
    hidden(1, 0)
    input_other(0)
    hidden(1, 1)
    input_other(1)
    input_own(0)
    d_first(0)
    g_second(0)
    release()
    gradient(1)
    g_middle(0)
    g_start(1)
    input_own(1)
    d_first(1)
    g_cross(0)
    d_second()
    g_middle_second(0)
    g_second(1)
    d_cross()
    g_final(0)
    g_middle(1)
    g_cross(1)
    newton(0)
    g_middle_second(1)
    d_final()
    g_final(1)
    for copy in backs:
        copy.wait()
    release()


def exchange(tokens, weight, cotangent, left_stats, right_stats):
    any_spec = pl.BlockSpec(memory_space=pl.ANY)
    vmem_spec = pl.BlockSpec(memory_space=pltpu.VMEM)
    dma = pltpu.SemaphoreType.DMA
    square = jax.ShapeDtypeStruct((BLK, BLK), F32)
    return pl.pallas_call(
        exchange_kernel,
        out_shape=(
            jax.ShapeDtypeStruct((TOK, FEAT), BF16),
            square,
            jax.ShapeDtypeStruct((BLK, BLK), BF16),
            square,
            square,
        ),
        in_specs=[any_spec] * 5,
        out_specs=(vmem_spec, vmem_spec, vmem_spec, any_spec, any_spec),
        scratch_shapes=[
            pltpu.VMEM((D, COLS), BF16),
            pltpu.VMEM((TOK, D), BF16),
            pltpu.VMEM((TOK, COLS), BF16),
            pltpu.VMEM((BLK, TOK), BF16),
            pltpu.VMEM((256, BLK), F32),
            pltpu.VMEM((2, 8, BLK, BLK), BF16),
            pltpu.VMEM((8, TOK, FEAT), BF16),
            pltpu.VMEM((2, 2, 2, XA[1], BLK), BF16),
            pltpu.VMEM((2, 2, ZA[1], BLK), BF16),
            pltpu.VMEM((2, 2, 2, 2, XA[1], BLK), BF16),
            pltpu.VMEM((2, 2, 2, ZA[1], BLK), BF16),
            pltpu.VMEM((2, 4, ZZ[1], BLK), BF16),
            pltpu.VMEM((2, 2, XA[1], BLK), BF16),
            pltpu.VMEM((8, TOK, FEAT), BF16),
            pltpu.VMEM((2, 2, TOK // 2, FEAT), BF16),
            pltpu.VMEM((2, 2, 2, TOK // 2, FEAT), BF16),
            pltpu.VMEM((2, TOK // 2, FEAT), BF16),
            pltpu.VMEM((BLK, BLK), F32),
            pltpu.VMEM((2, BLK, BLK), F32),
            pltpu.VMEM((2, BLK, BLK), F32),
            dma((N_SEND,)),
            dma((N_RECV,)),
            dma((7,)),
        ],
        compiler_params=pltpu.CompilerParams(
            collective_id=0, has_side_effects=True, vmem_limit_bytes=62 * 2**20
        ),
        cost_estimate=pl.CostEstimate(
            flops=6 * TOK * D * COLS, bytes_accessed=2**24, transcendentals=2 * TOK * COLS
        ),
        name="exchange",
    )(tokens, weight, cotangent, left_stats, right_stats)


def precondition_kernel(
    gt_ref, left_ref, right_ref, tg_ref, up_ref, lnew_ref, rnew_ref,
    tg_out, update_ref, left_out, right_out,
    up, lnew, rnew, tg_held, up_held, l_held, r_held, sems,
):
    def move(i, source, target):
        copy = pltpu.make_async_copy(source, target, sems.at[i])
        copy.start()
        return copy

    holds = (
        (tg_ref, tg_held, tg_out),
        (up_ref, up_held, update_ref.at[:, pl.ds(0, BLK)]),
        (lnew_ref, l_held, left_out.at[0, 0]),
        (rnew_ref, r_held, right_out.at[0, 0]),
    )
    olds = [
        move(11, left_ref.at[0, 1], lnew),
        move(12, right_ref.at[0, 1], rnew),
    ]
    arriving = [move(i, source, held) for i, (source, held, _) in enumerate(holds)]
    passed = []
    gt = gt_ref[...]
    grad = gt.T
    gth, gh = gt.astype(BF16), grad.astype(BF16)
    rows = lax.broadcasted_iota(jnp.int32, (BLK, BLK), 0)
    cols = lax.broadcasted_iota(jnp.int32, (BLK, BLK), 1)
    eye = jnp.where(rows == cols, 1.0, 0.0).astype(F32)
    share = (1.0 - decay_rate) / BLK
    left, right = share * dot(gh, gth), share * dot(gth, gh)
    for copy in olds:
        copy.wait()
    left = decay_rate * lnew[...] + left
    right = decay_rate * rnew[...] + right
    lnew[...] = left
    rnew[...] = right
    passed.append(move(4, lnew, left_out.at[0, 1]))
    passed.append(move(5, rnew, right_out.at[0, 1]))

    def each(function, *lists):
        return [function(*items) for items in zip(*lists)]

    def start(stat):
        trace = total_of(stat * eye)
        regular = stat + (ridge_share * trace / BLK) * eye
        scale = jnp.sqrt(total_of(regular * regular)) / 4.0
        return regular / scale, scale

    begun = each(start, (left, right))
    first = [b[0] for b in begun]
    scales = [b[1] for b in begun]
    firsth = each(lambda a: a.astype(BF16), first)
    square = each(dot, firsth, firsth)
    zero_sq = each(
        lambda a, q: (1.5625 * eye - 0.625 * a + 0.0625 * q).astype(BF16), first, square
    )
    crossed = each(lambda a, q: (1.25 * a - 0.25 * q).astype(BF16), first, square)
    fourth = each(lambda a: dot(a, a).astype(BF16), zero_sq)
    for i, (copy, (_, held, target)) in enumerate(zip(arriving, holds)):
        copy.wait()
        passed.append(move(7 + i, held, target))
    two = each(
        lambda a, f, x: 1.5625 * eye - 0.3125 * a - 0.25 * dot(f, x), first, fourth, crossed
    )
    twoh = each(lambda a: a.astype(BF16), two)
    two_sq = each(lambda a: dot(a, a).astype(BF16), twoh)
    two_crossed = each(lambda a, f: dot(a, f).astype(BF16), twoh, firsth)
    two_fourth = each(lambda a: dot(a, a).astype(BF16), two_sq)
    roots = each(
        lambda a, f, x, s: (
            lax.rsqrt(jnp.sqrt(s)) * (1.25 * a - 0.25 * dot(f, x))
        ).astype(BF16),
        two, two_fourth, two_crossed, scales,
    )
    left_part = dot(roots[0], gh).astype(BF16)
    raw = dot(left_part, roots[1])
    size = float(BLK * BLK)
    grad_rms = jnp.sqrt(total_of(gt * gt) / size)
    raw_rms = jnp.sqrt(total_of(raw * raw) / size + epsilon)
    up[...] = (raw * (grad_rms / raw_rms)).astype(BF16)
    passed.append(move(6, up, update_ref.at[:, pl.ds(BLK, BLK)]))
    for copy in passed:
        copy.wait()


def precondition(gt, left_stats, right_stats, tokens_grad, up, left_new, right_new):
    any_spec = pl.BlockSpec(memory_space=pl.ANY)
    return pl.pallas_call(
        precondition_kernel,
        grid=(1,),
        out_shape=(
            jax.ShapeDtypeStruct((TOK, FEAT), BF16),
            jax.ShapeDtypeStruct((BLK, COLS), BF16),
            jax.ShapeDtypeStruct(left_stats.shape, F32),
            jax.ShapeDtypeStruct(right_stats.shape, F32),
        ),
        in_specs=[pl.BlockSpec((BLK, BLK), lambda i: (0, 0))] + [any_spec] * 6,
        out_specs=(any_spec,) * 4,
        scratch_shapes=[
            pltpu.VMEM((BLK, BLK), BF16),
            pltpu.VMEM((BLK, BLK), F32),
            pltpu.VMEM((BLK, BLK), F32),
            pltpu.VMEM((TOK, FEAT), BF16),
            pltpu.VMEM((BLK, BLK), BF16),
            pltpu.VMEM((BLK, BLK), F32),
            pltpu.VMEM((BLK, BLK), F32),
            pltpu.SemaphoreType.DMA((13,)),
        ],
        compiler_params=pltpu.CompilerParams(vmem_limit_bytes=62 * 2**20),
        name="precondition",
    )(gt, left_stats, right_stats, tokens_grad, up, left_new, right_new)


def shards(tokens, weight, cotangent, left_stats, right_stats):
    tokens_grad, gt, up, left_half, right_half = exchange(
        tokens, weight, cotangent, left_stats, right_stats
    )
    return precondition(gt, left_stats, right_stats, tokens_grad, up, left_half, right_half)


def solution(mesh):
    two = P("dp", ("tensor", "pre"))
    four = P("dp", ("tensor", "pre"), None, None)
    return jax.shard_map(
        shards,
        mesh=mesh,
        in_specs=(two, two, two, four, four),
        out_specs=(two, two, four, four),
        check_vma=False,
    )
```
